32 devices in a mesh: segment: 2 (over core), expert: 4 (over z), pair: 4 (over y, x).
Axes of the slice: x: 2, y: 2, z: 4, core: 2. Of those that a mesh axis runs over, the one named last changes fastest.
Arguments:
- acts: bfloat16 [2, 2, 768, 768], P(None, None, 'expert', 'pair'), may hold values from -20 to 20
- cotangent: bfloat16 [2, 768, 768], P(None, 'expert', 'pair'), may hold values from -6 to 6
- gates: float32 [2, 2, 768], P(None, None, 'expert'), may hold values from 0.2 to 1
- owners: int32 [2, 2, 768], P(None, None, 'expert'), may hold values from 0 to 3, as said below
- slots: int32 [2, 2, 768], P(None, None, 'expert'), may hold values from 0 to 59
- w_in: bfloat16 [2, 4, 768, 3072], P('segment', 'expert', None, 'pair'), may hold values from -0.21875 to 0.21875
- w_out: bfloat16 [2, 4, 3072, 768], P('segment', 'expert', 'pair'), may hold values from -0.109375 to 0.109375
Outputs:
- grads: bfloat16 [2, 2, 768, 768], P('segment', None, 'expert', 'pair')
- grad_in: bfloat16 [2, 4, 768, 3072], P('segment', 'expert', None, 'pair')
- grad_out: bfloat16 [2, 4, 3072, 768], P('segment', 'expert', 'pair')
The draws below stay inside these ranges and needn't reach their ends.
Inputs may be any that keep to these rules, and one draw needn't show every extreme that they name: `owners`: within each aligned block of 192 tokens of one sublayer and micro-batch, no two tokens share both owner and slot. One expert, the same for all blocks of a draw, takes exactly 60 tokens of every block.
All inputs are finite; a program needn't handle non-finite values.
Results may differ from the reference program's by a relative error of at most 0.02.
Values may be sent and summed in bfloat16 or wider, within the bound.
A program may use at most 64 MiB of HBM per device.

```python
import math
import jax
import jax.numpy as jnp
from jax import lax

D = 768
FF = 3072
TOK_DEV = 192
MICRO = 2
EXPERTS = 4
CAP = 60
TOKENS = 768
N_PAIR = 4


def routing(key):
    block_count = 2 * MICRO * (TOKENS // TOK_DEV)
    keys = jax.random.split(key, block_count + 1)
    favored = jax.random.randint(keys[0], (), 0, EXPERTS).astype(jnp.int32)

    def one_block(block_key):
        first_key, second_key = jax.random.split(block_key)
        chosen = jax.random.permutation(first_key, (EXPERTS - 1) * CAP)[:TOK_DEV - CAP].astype(jnp.int32)
        others = chosen // CAP
        owner_part = others + (others >= favored).astype(jnp.int32)
        slot_part = chosen % CAP
        owner_all = jnp.concatenate([jnp.full((CAP,), favored, jnp.int32), owner_part])
        slot_all = jnp.concatenate([jnp.arange(CAP, dtype=jnp.int32), slot_part])
        order = jax.random.permutation(second_key, TOK_DEV)
        return (owner_all[order], slot_all[order])
    owner_blocks, slot_blocks = jax.vmap(one_block)(keys[1:])
    return (owner_blocks.reshape(2, MICRO, TOKENS).astype(jnp.int32), slot_blocks.reshape(2, MICRO, TOKENS).astype(jnp.int32))


def draw_owners(key, part):
    return routing(key)[0]


def draw_slots(key, part):
    return routing(key)[1]


def draw_acts(key, part):
    key = jax.random.fold_in(key, 7)
    base_key, row_key, col_key = jax.random.split(key, 3)
    shape = (2, MICRO, TOKENS, D)
    row_scale = jnp.exp(jax.random.uniform(row_key, (2, MICRO, TOKENS, 1), jnp.float32, 0.0, math.log(10.0)))
    col_scale = jnp.exp(jax.random.uniform(col_key, (2, 1, 1, D), jnp.float32, 0.0, math.log(10.0)))
    base = jax.random.normal(base_key, shape, jnp.float32)
    base = jnp.clip(base, -4.0, 4.0)
    return (base * row_scale * col_scale / 20.0).astype(jnp.bfloat16)


def block_scale(key, dims, cuts, least, largest):
    level = 1.0
    for dim, blocks in cuts:
        steps = jax.random.uniform(jax.random.fold_in(jax.random.fold_in(key, 6), dim), (blocks,), jnp.float32, least / len(cuts), largest / len(cuts))
        level = level * jnp.repeat(jnp.exp(steps), dims[dim] // blocks).reshape((-1,) + (1,) * (len(dims) - 1 - dim))
    return level


def normal_values(stream_key, extent, spread, most, cuts=(), kind=jnp.bfloat16):
    factor_of = block_scale(stream_key, extent, cuts, -0.22, 0.18) if cuts else 1.0
    values = jax.random.normal(stream_key, extent, jnp.float32) * spread * factor_of
    return jnp.minimum(jnp.maximum(values, -most), most).astype(kind)


def setup_inputs(seed: int = 0) -> dict:
    key_list = jax.random.split(jax.random.key(seed), 8)
    return {
        "acts": draw_acts(jax.random.fold_in(key_list[7], 71), 0),
        "cotangent": normal_values(key_list[1], (MICRO, TOKENS, D), 1.0, 6.0, ((1, 4), (2, 4))),
        "gates": jnp.clip(0.2 + 0.8 * jax.random.uniform(key_list[2], (2, MICRO, TOKENS), jnp.float32) ** block_scale(key_list[2], (2, MICRO, TOKENS), ((2, 4),), -0.2, 0.2), 0.2, 1.0),
        "owners": draw_owners(jax.random.fold_in(key_list[7], 71), 0),
        "slots": draw_slots(jax.random.fold_in(key_list[7], 71), 0),
        "w_in": normal_values(key_list[5], (2, EXPERTS, D, FF), D ** -0.5, 0.21875, ((0, 2), (1, 4), (3, 4))),
        "w_out": normal_values(key_list[6], (2, EXPERTS, FF, D), FF ** -0.5, 0.109375, ((0, 2), (1, 4), (2, 4))),
    }


def gelu_value(pre_act):
    inner_arg = 0.7978845608 * (pre_act + 0.044715 * pre_act * pre_act * pre_act)
    return 0.5 * pre_act * (1.0 + jnp.tanh(inner_arg))

def gelu_slope(pre_act):
    inner_arg = 0.7978845608 * (pre_act + 0.044715 * pre_act * pre_act * pre_act)
    tangent = jnp.tanh(inner_arg)
    return 0.5 * (1.0 + tangent) + 0.5 * pre_act * (1.0 - tangent * tangent) * 0.7978845608 * (1.0 + 0.134145 * pre_act * pre_act)

def layer_reference(layer_acts, upstream, gate_row, owner_row, slot_row, first_weights, second_weights):
    act_float = layer_acts.astype(jnp.float32)
    scale_inv = lax.rsqrt(lax.optimization_barrier(jnp.mean(act_float * act_float, axis=1)) + 1e-06)
    normed = (act_float * scale_inv[:, None]).astype(jnp.bfloat16)
    scaled = (gate_row[:, None] * upstream.astype(jnp.float32)).astype(jnp.bfloat16)
    source_block = (jnp.arange(TOKENS) // TOK_DEV).astype(jnp.int32)
    position = source_block * CAP + slot_row.astype(jnp.int32)
    slot_total = TOKENS // TOK_DEV * CAP
    expert_in = jnp.zeros((EXPERTS, slot_total, D), jnp.bfloat16).at[owner_row, position].set(normed)
    expert_grad = jnp.zeros((EXPERTS, slot_total, D), jnp.bfloat16).at[owner_row, position].set(scaled)
    block_count = 2 * N_PAIR

    def per_expert(operands):
        rows_in, rows_grad, weight_first, weight_second = operands
        pre_act = jnp.dot(rows_in, weight_first, preferred_element_type=jnp.float32)
        hidden = gelu_value(pre_act).astype(jnp.bfloat16)
        back_hidden = jnp.dot(rows_grad, weight_second.T, preferred_element_type=jnp.float32)
        back_pre = (back_hidden * gelu_slope(pre_act)).astype(jnp.bfloat16)
        grad_first = jnp.dot(rows_in.T, back_pre, preferred_element_type=jnp.float32)
        grad_second = jnp.dot(hidden.T, rows_grad, preferred_element_type=jnp.float32)
        blocks = back_pre.astype(jnp.float32).reshape(slot_total, block_count, FF // block_count)
        weight_blocks = weight_first.astype(jnp.float32).reshape(D, block_count, FF // block_count)
        partials = jnp.einsum('rpf,dpf->prd', blocks, weight_blocks)
        summed = lax.optimization_barrier(jnp.sum(partials.astype(jnp.bfloat16).astype(jnp.float32), axis=0))
        return (grad_first, grad_second, summed)
    grad_first, grad_second, summed = lax.map(per_expert, (expert_in, expert_grad, first_weights, second_weights))
    arrived = summed[owner_row, position]
    inner = lax.optimization_barrier(jnp.sum(arrived * act_float, axis=1))
    branch = (scale_inv[:, None] * arrived - (scale_inv ** 3 * inner / D)[:, None] * act_float).astype(jnp.bfloat16)
    result = (upstream.astype(jnp.float32) + branch.astype(jnp.float32)).astype(jnp.bfloat16)
    return (result, grad_first, grad_second)

def reference(acts, cotangent, gates, owners, slots, w_in, w_out):
    upper_list = []
    lower_list = []
    upper_first = jnp.zeros((EXPERTS, D, FF), jnp.float32)
    upper_second = jnp.zeros((EXPERTS, FF, D), jnp.float32)
    lower_first = jnp.zeros((EXPERTS, D, FF), jnp.float32)
    lower_second = jnp.zeros((EXPERTS, FF, D), jnp.float32)
    for micro_index in range(MICRO):
        upper, first_term, second_term = layer_reference(acts[1, micro_index], cotangent[micro_index], gates[1, micro_index], owners[1, micro_index], slots[1, micro_index], w_in[1], w_out[1])
        upper_first = upper_first + first_term
        upper_second = upper_second + second_term
        lower, first_term, second_term = layer_reference(acts[0, micro_index], upper, gates[0, micro_index], owners[0, micro_index], slots[0, micro_index], w_in[0], w_out[0])
        lower_first = lower_first + first_term
        lower_second = lower_second + second_term
        upper_list.append(upper)
        lower_list.append(lower)
    grads = jnp.stack([jnp.stack(lower_list), jnp.stack(upper_list)])
    grad_in = jnp.stack([lower_first, upper_first]).astype(jnp.bfloat16)
    grad_out = jnp.stack([lower_second, upper_second]).astype(jnp.bfloat16)
    return (grads, grad_in, grad_out)
```

```python
import functools

import jax
import jax.numpy as jnp
from jax import lax
from jax.experimental import pallas as pl
from jax.experimental.pallas import tpu as pltpu
from jax.sharding import PartitionSpec as P

BF = jnp.bfloat16
F32 = jnp.float32
MESH = pl.DeviceIdType.MESH


def repeat(count, step):
    if count <= 4:
        for i in range(count):
            step(i)
    else:
        lax.fori_loop(0, count, lambda i, c: (step(i), c)[1], 0)


def dot(a, b, ca, cb):
    return lax.dot_general(a, b, (((ca,), (cb,)), ((), ())), preferred_element_type=F32)


def eye(n):
    return lax.broadcasted_iota(jnp.int32, (n, n), 0) == lax.broadcasted_iota(jnp.int32, (n, n), 1)


def as_column(row):
    return jnp.sum(jnp.where(eye(row.shape[1]), row, 0.0), axis=1, keepdims=True)


def as_row(column):
    return jnp.sum(jnp.where(eye(column.shape[0]), column, 0.0), axis=0, keepdims=True)


def kernel(
    E, PN, cap, acts, cot, gates, owners, slots, win_h, wout_h, grads, gin_h, gout_h,
    win, wout, gin, gout, placing, zs_a, zs_g, gat_a, gat_g, xn, xg, inv_s, pre_s, slope_s, hid_s, bp_s,
    s_s, s_r, rs_s, rs_r, ret_s, ret_r, up_r,
    zsem_a, zrec_a, zsem_g, zrec_g, psem_a, prec_a, psem_g, prec_g,
    ssem, srec, rsem, rrec, tsem, trec, upsem, uprec, lsem,
):
    seg = lax.axis_index("segment")
    me = lax.axis_index("expert")
    mp = lax.axis_index("pair")
    M, T, F = cot.shape
    D = F * PN
    H = win.shape[1]
    R = E * cap
    B = M * cap
    groups = min(E, 4)
    ge = E // groups
    mg = me // ge

    load_in = pltpu.make_async_copy(win_h.at[0, 0], win, lsem.at[0])
    load_out = pltpu.make_async_copy(wout_h.at[0, 0], wout, lsem.at[1])
    load_in.start()
    load_out.start()

    barrier = pltpu.get_barrier_semaphore()

    def greet_e(k):
        pl.semaphore_signal(barrier, inc=1, device_id={"expert": lax.rem(me + k + 1, E)}, device_id_type=MESH)

    repeat(E - 1, greet_e)
    for k in range(1, PN):
        pl.semaphore_signal(barrier, inc=1, device_id={"pair": lax.rem(mp + k, PN)}, device_id_type=MESH)
    pl.semaphore_signal(barrier, inc=1, device_id={"segment": 1 - seg}, device_id_type=MESH)

    for m in range(M):
        target = owners[seg, pl.ds(m, 1), :] * cap + slots[seg, pl.ds(m, 1), :]
        placing[m] = (lax.broadcasted_iota(jnp.int32, (R, T), 0) == target).astype(BF)

    def pack(values, zs):
        rows = [dot(placing[m], values[m], 1, 0) for m in range(M)]
        zs[...] = jnp.concatenate(rows, axis=1).astype(BF).reshape(E, cap, M * F)

    def z_copy(zs, gat, ssems, rsems, d, src):
        return pltpu.make_async_remote_copy(
            src_ref=zs.at[d], dst_ref=gat.at[mp, src], send_sem=ssems.at[d], recv_sem=rsems.at[src],
            device_id={"expert": d}, device_id_type=MESH)

    def send_z(zs, gat, ssems, rsems):
        repeat(E - 1, lambda k: z_copy(zs, gat, ssems, rsems, lax.rem(me + k + 1, E), me).start())
        gat[mp, me] = zs[me]

    def p_copy(gat, ssems, rsems, q, src, g):
        part = gat.at[src, pl.ds(g * ge, ge)]
        return pltpu.make_async_remote_copy(
            src_ref=part, dst_ref=part, send_sem=ssems.at[q, g], recv_sem=rsems.at[src, g],
            device_id={"pair": q}, device_id_type=MESH)

    def forward(zs, gat, zsems, zrecs, psems, precs):
        def one(j):
            g = lax.rem(mg + j, groups)

            def arrive(i):
                e = g * ge + i

                @pl.when(e != me)
                def _():
                    z_copy(zs, gat, zsems, zrecs, e, e).wait_recv()

            repeat(ge, arrive)
            for k in range(1, PN):
                p_copy(gat, psems, precs, lax.rem(mp + k, PN), mp, g).start()

        repeat(groups, one)

    def gathered(gat, psems, precs, j):
        g = lax.rem(mg + j, groups)
        for k in range(1, PN):
            q = lax.rem(mp + k, PN)
            p_copy(gat, psems, precs, q, q, g).wait_recv()
        return g

    def finish(zs, gat, zsems, zrecs, psems, precs):
        repeat(E - 1, lambda k: z_copy(zs, gat, zsems, zrecs, lax.rem(me + k + 1, E), me).wait_send())

        def one(g):
            for k in range(1, PN):
                p_copy(gat, psems, precs, lax.rem(mp + k, PN), mp, g).wait_send()

        repeat(groups, one)

    a_set = (zs_a, gat_a, zsem_a, zrec_a, psem_a, prec_a)
    g_set = (zs_g, gat_g, zsem_g, zrec_g, psem_g, prec_g)

    pack([acts[seg, m] for m in range(M)], zs_a)
    pl.semaphore_wait(barrier, E - 1 + PN - 1 + 1)
    send_z(zs_a, gat_a, zsem_a, zrec_a)

    def send_grad():
        scaled = []
        for m in range(M):
            gate = as_column(gates[seg, pl.ds(m, 1), :])
            scaled.append((gate * up_r[m].astype(F32)).astype(BF))
        pack(scaled, zs_g)
        send_z(zs_g, gat_g, zsem_g, zrec_g)

    @pl.when(seg == 1)
    def _():
        up_r[...] = cot[...]
        send_grad()

    forward(*a_set)

    @pl.when(seg == 1)
    def _():
        forward(*g_set)

    def take_acts(j):
        g = gathered(gat_a, psem_a, prec_a, j)

        def block(i):
            e = g * ge + i
            parts = [gat_a[q, e].astype(F32) for q in range(PN)]
            for m in range(M):
                full = jnp.concatenate([v[:, m * F:(m + 1) * F] for v in parts], axis=1)
                scale = lax.rsqrt(jnp.mean(full * full, axis=1, keepdims=True) + 1e-06)
                rows = pl.ds(pl.multiple_of(e * B + m * cap, 16), cap)
                inv_s[rows, :] = scale
                xn[rows, :] = (full * scale).astype(BF)

        repeat(ge, block)

    repeat(groups, take_acts)
    load_in.wait()
    tile = 256 if H % 256 == 0 else 128
    chunk = min(M * R, 512)

    def tiles(step):
        def both(i):
            row = pl.ds(pl.multiple_of((i // (H // tile)) * chunk, 16), chunk)
            col = pl.ds(pl.multiple_of((i % (H // tile)) * tile, 128), tile)
            step(row, col)

        repeat((M * R // chunk) * (H // tile), both)

    def pre_step(row, col):
        u = dot(xn[row, :], win[:, col], 1, 0)
        square = u * u
        tangent = jnp.tanh(0.7978845608 * (u + 0.044715 * square * u))
        pre_s[row, col] = u
        hid_s[row, col] = (0.5 * u * (1.0 + tangent)).astype(BF)
        slope_s[row, col] = 0.5 * (1.0 + tangent) + 0.5 * u * (1.0 - tangent * tangent) * 0.7978845608 * (
            1.0 + 0.134145 * square)

    tiles(pre_step)
    load_out.wait()

    def up_copy():
        return pltpu.make_async_remote_copy(
            src_ref=grads.at[0], dst_ref=up_r, send_sem=upsem, recv_sem=uprec,
            device_id={"segment": 1 - seg}, device_id_type=MESH)

    @pl.when(seg == 0)
    def _():
        up_copy().wait_recv()
        send_grad()
        forward(*g_set)

    def take_grads(j):
        g = gathered(gat_g, psem_g, prec_g, j)

        def block(i):
            e = g * ge + i
            parts = [gat_g[q, e].astype(F32) for q in range(PN)]
            for m in range(M):
                full = jnp.concatenate([v[:, m * F:(m + 1) * F] for v in parts], axis=1)
                xg[pl.ds(pl.multiple_of(e * B + m * cap, 16), cap), :] = full.astype(BF)

        repeat(ge, block)

    repeat(groups, take_grads)

    def back_step(row, col):
        back = dot(xg[row, :], wout[col, :], 1, 1)
        bp_s[row, col] = (back * slope_s[row, col]).astype(BF)

    tiles(back_step)

    def r_copy(q, src, g):
        rows = pl.ds(g * ge, ge)
        return pltpu.make_async_remote_copy(
            src_ref=rs_s.at[q, rows], dst_ref=rs_r.at[src, rows], send_sem=rsem.at[q, g], recv_sem=rrec.at[src, g],
            device_id={"pair": q}, device_id_type=MESH)

    def s_copy(q, src):
        return pltpu.make_async_remote_copy(
            src_ref=s_s, dst_ref=s_r.at[src], send_sem=ssem.at[q], recv_sem=srec.at[src],
            device_id={"pair": q}, device_id_type=MESH)

    def partial_for(q, out):
        weights = win[pl.ds(pl.multiple_of(q * F, 16), F), :]

        def rows_step(i):
            part = dot(bp_s[pl.ds(pl.multiple_of(i * chunk, 16), chunk), :], weights, 1, 1)
            blocks = part.reshape(chunk // B, M, cap, F)
            joined = jnp.concatenate([blocks[:, m] for m in range(M)], axis=-1)
            out[q, pl.ds(i * (chunk // B), chunk // B)] = joined.astype(BF)

        repeat(M * R // chunk, rows_step)

    for k in range(1, PN):
        q = lax.rem(mp + k, PN)
        partial_for(q, rs_s)
        repeat(groups, lambda j: r_copy(q, mp, lax.rem(mg + 1 + j, groups)).start())

    def inner_step(e):
        rows = pl.ds(pl.multiple_of(e * B, 16), B)
        s_s[e] = as_row(jnp.sum(bp_s[rows, :].astype(F32) * pre_s[rows, :], axis=1, keepdims=True))

    repeat(E, inner_step)
    for k in range(1, PN):
        s_copy(lax.rem(mp + k, PN), mp).start()
    s_r[mp] = s_s[...]
    partial_for(mp, rs_r)

    def weight_grads():
        def one(i):
            col = pl.ds(pl.multiple_of(i * tile, 128), tile)
            gin[:, col] = dot(xn[...], bp_s[:, col], 0, 0).astype(BF)
            gout[col, :] = dot(hid_s[:, col], xg[...], 0, 0).astype(BF)

        repeat(H // tile, one)

    weight_grads()
    put_in = pltpu.make_async_copy(gin, gin_h.at[0, 0], lsem.at[2])
    put_out = pltpu.make_async_copy(gout, gout_h.at[0, 0], lsem.at[3])
    put_in.start()
    put_out.start()

    def t_copy(d, src):
        return pltpu.make_async_remote_copy(
            src_ref=ret_s.at[d], dst_ref=ret_r.at[src], send_sem=tsem.at[d], recv_sem=trec.at[src],
            device_id={"expert": d}, device_id_type=MESH)

    for k in range(1, PN):
        q = lax.rem(mp + k, PN)
        s_copy(q, q).wait_recv()

    def give_back(j):
        g = lax.rem(mg + 1 + j, groups)
        for k in range(1, PN):
            q = lax.rem(mp + k, PN)
            r_copy(q, q, g).wait_recv()

        def block(i):
            e = g * ge + i
            total = rs_r[0, e].astype(F32)
            inner = s_r[0, e]
            for q in range(1, PN):
                total = total + rs_r[q, e].astype(F32)
                inner = inner + s_r[q, e]
            inner = as_column(inner)
            own = gat_a[mp, e].astype(F32)
            pieces = []
            for m in range(M):
                scale = inv_s[pl.ds(pl.multiple_of(e * B + m * cap, 16), cap), :]
                lanes = slice(m * F, (m + 1) * F)
                factor = scale * scale * inner[m * cap:(m + 1) * cap] / D
                pieces.append(scale * total[:, lanes] - factor * own[:, lanes])
            ret_s[e] = jnp.concatenate(pieces, axis=1).astype(BF)

            @pl.when(e != me)
            def _():
                t_copy(e, me).start()

        repeat(ge, block)

    repeat(groups, give_back)
    ret_r[me] = ret_s[me]

    def back_arrive(k):
        src = lax.rem(me + k + 1, E)
        t_copy(src, src).wait_recv()

    repeat(E - 1, back_arrive)
    returned = ret_r[...].reshape(R, M * F)
    for m in range(M):
        restored = dot(placing[m], returned[:, m * F:(m + 1) * F], 0, 0)
        grads[0, m] = (up_r[m].astype(F32) + restored).astype(BF)

    @pl.when(seg == 1)
    def _():
        up_copy().start()

    finish(*a_set)
    finish(*g_set)
    for k in range(1, PN):
        q = lax.rem(mp + k, PN)
        s_copy(q, mp).wait_send()
        repeat(groups, lambda g: r_copy(q, mp, g).wait_send())
    repeat(E - 1, lambda k: t_copy(lax.rem(me + k + 1, E), me).wait_send())
    put_in.wait()
    put_out.wait()

    @pl.when(seg == 1)
    def _():
        up_copy().wait_send()


def body(acts, cotangent, gates, owners, slots, w_in, w_out):
    E = lax.axis_size("expert")
    PN = lax.axis_size("pair")
    M, T, F = cotangent.shape
    D, H = w_in.shape[2:]
    capacity = max(2, (5 * T + 4 * E - 1) // (4 * E))
    cap = (capacity + 15) // 16 * 16
    R = E * cap
    W = M * F
    groups = min(E, 4)
    vm = pltpu.VMEM
    dma = pltpu.SemaphoreType.DMA
    scratch = [
        vm((D, H), BF), vm((H, D), BF), vm((D, H), BF), vm((H, D), BF),
        vm((M, R, T), BF), vm((E, cap, W), BF), vm((E, cap, W), BF),
        vm((PN, E, cap, W), BF), vm((PN, E, cap, W), BF),
        vm((M * R, D), BF), vm((M * R, D), BF), vm((M * R, 1), F32),
        vm((M * R, H), F32), vm((M * R, H), F32), vm((M * R, H), BF), vm((M * R, H), BF),
        vm((E, 1, M * cap), F32), vm((PN, E, 1, M * cap), F32),
        vm((PN, E, cap, W), BF), vm((PN, E, cap, W), BF),
        vm((E, cap, W), BF), vm((E, cap, W), BF), vm((M, T, F), BF),
        dma((E,)), dma((E,)), dma((E,)), dma((E,)),
        dma((PN, groups)), dma((PN, groups)), dma((PN, groups)), dma((PN, groups)),
        dma((PN,)), dma((PN,)), dma((PN, groups)), dma((PN, groups)),
        dma((E,)), dma((E,)), dma(()), dma(()), dma((4,)),
    ]
    whole = pl.BlockSpec(memory_space=pltpu.VMEM)
    away = pl.BlockSpec(memory_space=pl.ANY)
    return pl.pallas_call(
        functools.partial(kernel, E, PN, cap),
        out_shape=(
            jax.ShapeDtypeStruct((1, M, T, F), BF),
            jax.ShapeDtypeStruct((1, 1, D, H), BF),
            jax.ShapeDtypeStruct((1, 1, H, D), BF),
        ),
        in_specs=[whole] * 5 + [away] * 2,
        out_specs=(whole, away, away),
        scratch_shapes=scratch,
        compiler_params=pltpu.CompilerParams(
            collective_id=0, has_side_effects=True, vmem_limit_bytes=56 * 1024 * 1024),
        cost_estimate=pl.CostEstimate(
            flops=10 * M * R * D * H, bytes_accessed=8 * D * H, transcendentals=M * R * H),
    )(acts, cotangent, gates, owners, slots, w_in, w_out)


def solution(mesh):
    placed = (
        P(None, None, "expert", "pair"),
        P(None, "expert", "pair"),
        P(None, None, "expert"),
        P(None, None, "expert"),
        P(None, None, "expert"),
        P("segment", "expert", None, "pair"),
        P("segment", "expert", "pair", None),
    )
    return jax.shard_map(
        body,
        mesh=mesh,
        in_specs=placed,
        out_specs=(
            P("segment", None, "expert", "pair"),
            P("segment", "expert", None, "pair"),
            P("segment", "expert", "pair", None),
        ),
        check_vma=False,
    )
```

```python
import functools

import jax
import jax.numpy as jnp
from jax import lax
from jax.experimental import pallas as pl
from jax.experimental.pallas import tpu as pltpu
from jax.sharding import PartitionSpec as P

BF = jnp.bfloat16
F32 = jnp.float32
MESH = pl.DeviceIdType.MESH


def repeat(count, step):
    if count <= 4:
        for i in range(count):
            step(i)
    else:
        lax.fori_loop(0, count, lambda i, c: (step(i), c)[1], 0)


def dot(a, b, ca, cb):
    return lax.dot_general(a, b, (((ca,), (cb,)), ((), ())), preferred_element_type=F32)


def eye(n):
    return lax.broadcasted_iota(jnp.int32, (n, n), 0) == lax.broadcasted_iota(jnp.int32, (n, n), 1)


def as_column(row):
    return jnp.sum(jnp.where(eye(row.shape[1]), row, 0.0), axis=1, keepdims=True)


def as_row(column):
    return jnp.sum(jnp.where(eye(column.shape[0]), column, 0.0), axis=0, keepdims=True)


def kernel(
    E, PN, cap, acts, cot, gates, owners, slots, win_h, wout_h, grads, gin_h, gout_h,
    win, wout, gin, gout, placing, zs_a, zs_g, gat_a, gat_g, xn, xg, inv_s, pre_s, slope_s, hid_s, bp_s,
    s_s, s_r, rs_s, rs_r, ret_s, ret_r, up_r, gate_s, inner_s,
    zsem_a, zrec_a, zsem_g, zrec_g, psem_a, prec_a, psem_g, prec_g,
    ssem, srec, rsem, rrec, tsem, trec, upsem, uprec, lsem, go_sem,
):
    seg = lax.axis_index("segment")
    me = lax.axis_index("expert")
    mp = lax.axis_index("pair")
    M, T, F = cot.shape
    D = F * PN
    H = win.shape[1]
    R = E * cap
    B = M * cap
    groups = min(E, 4)
    ge = E // groups
    mg = me // ge

    load_in = pltpu.make_async_copy(win_h.at[0, 0], win, lsem.at[0])
    load_out = pltpu.make_async_copy(wout_h.at[0, 0], wout, lsem.at[1])
    load_in.start()
    load_out.start()

    barrier = pltpu.get_barrier_semaphore()

    def greet_e(k):
        pl.semaphore_signal(barrier, inc=1, device_id={"expert": lax.rem(me + k + 1, E)}, device_id_type=MESH)

    repeat(E - 1, greet_e)
    for k in range(1, PN):
        pl.semaphore_signal(barrier, inc=1, device_id={"pair": lax.rem(mp + k, PN)}, device_id_type=MESH)
    pl.semaphore_signal(barrier, inc=1, device_id={"segment": 1 - seg}, device_id_type=MESH)

    for m in range(M):
        target = owners[seg, pl.ds(m, 1), :] * cap + slots[seg, pl.ds(m, 1), :]
        placing[m] = (lax.broadcasted_iota(jnp.int32, (R, T), 0) == target).astype(BF)

    def pack(values, zs):
        rows = [dot(placing[m], values[m], 1, 0) for m in range(M)]
        zs[...] = jnp.concatenate(rows, axis=1).astype(BF).reshape(E, cap, M * F)

    def z_copy(zs, gat, ssems, rsems, d, src):
        return pltpu.make_async_remote_copy(
            src_ref=zs.at[d], dst_ref=gat.at[mp, src], send_sem=ssems.at[d], recv_sem=rsems.at[src],
            device_id={"expert": d}, device_id_type=MESH)

    def send_z(zs, gat, ssems, rsems):
        repeat(E - 1, lambda k: z_copy(zs, gat, ssems, rsems, lax.rem(me + k + 1, E), me).start())
        gat[mp, me] = zs[me]

    def p_copy(gat, ssems, rsems, q, src, g):
        part = gat.at[src, pl.ds(g * ge, ge)]
        return pltpu.make_async_remote_copy(
            src_ref=part, dst_ref=part, send_sem=ssems.at[q, g], recv_sem=rsems.at[src, g],
            device_id={"pair": q}, device_id_type=MESH)

    def forward(zs, gat, zsems, zrecs, psems, precs, j):
        g = lax.rem(mg + groups - j, groups)

        def arrive(i):
            e = g * ge + i

            @pl.when(e != me)
            def _():
                z_copy(zs, gat, zsems, zrecs, e, e).wait_recv()

        repeat(ge, arrive)
        for k in range(PN - 1, 0, -1):
            p_copy(gat, psems, precs, lax.rem(mp + k, PN), mp, g).start()

    def gathered(gat, psems, precs, j):
        g = lax.rem(mg + groups - j, groups)
        for k in range(1, PN):
            q = lax.rem(mp + k, PN)
            p_copy(gat, psems, precs, q, q, g).wait_recv()
        return g

    def finish(zs, gat, zsems, zrecs, psems, precs):
        repeat(E - 1, lambda k: z_copy(zs, gat, zsems, zrecs, lax.rem(me + k + 1, E), me).wait_send())

        def one(g):
            for k in range(1, PN):
                p_copy(gat, psems, precs, lax.rem(mp + k, PN), mp, g).wait_send()

        repeat(groups, one)

    a_set = (zs_a, gat_a, zsem_a, zrec_a, psem_a, prec_a)
    g_set = (zs_g, gat_g, zsem_g, zrec_g, psem_g, prec_g)
    unit = ge * B

    def go(i):
        pl.semaphore_signal(go_sem.at[i], inc=1, device_id={"segment": 1 - seg}, device_id_type=MESH)

    def send_grad():
        scaled = [(gate_s[m] * up_r[m].astype(F32)).astype(BF) for m in range(M)]
        pack(scaled, zs_g)
        send_z(zs_g, gat_g, zsem_g, zrec_g)

    def take(gat, psems, precs, j, use):
        g = gathered(gat, psems, precs, j)

        def block(i):
            e = g * ge + i
            parts = [gat[q, e].astype(F32) for q in range(PN)]
            for m in range(M):
                full = jnp.concatenate([v[:, m * F:(m + 1) * F] for v in parts], axis=1)
                use(pl.ds(pl.multiple_of(e * B + m * cap, 16), cap), full)

        repeat(ge, block)
        return g, pl.ds(pl.multiple_of(g * unit, 16), unit)

    def norm_rows(rows, full):
        scale = lax.rsqrt(jnp.mean(full * full, axis=1, keepdims=True) + 1e-06)
        inv_s[rows, :] = scale
        xn[rows, :] = (full * scale).astype(BF)

    def grad_rows(rows, full):
        xg[rows, :] = full.astype(BF)

    def r_copy(q, src, g):
        rows = pl.ds(g * ge, ge)
        return pltpu.make_async_remote_copy(
            src_ref=rs_s.at[q, rows], dst_ref=rs_r.at[src, rows], send_sem=rsem.at[q, g], recv_sem=rrec.at[src, g],
            device_id={"pair": q}, device_id_type=MESH)

    def s_copy(q, src, g):
        rows = pl.ds(g * ge, ge)
        return pltpu.make_async_remote_copy(
            src_ref=s_s.at[rows], dst_ref=s_r.at[src, rows], send_sem=ssem.at[q, g], recv_sem=srec.at[src, g],
            device_id={"pair": q}, device_id_type=MESH)

    def forward_pass(j):
        _, rows = take(gat_a, psem_a, prec_a, j, norm_rows)
        for t in range(H // tile):
            col = pl.ds(t * tile, tile)
            u = dot(xn[rows, :], win[:, col], 1, 0)
            square = u * u
            tangent = jnp.tanh(0.7978845608 * (u + 0.044715 * square * u))
            pre_s[rows, col] = u
            hid_s[rows, col] = (0.5 * u * (1.0 + tangent)).astype(BF)
            slope_s[rows, col] = 0.5 * (1.0 + tangent) + 0.5 * u * (1.0 - tangent * tangent) * 0.7978845608 * (
                1.0 + 0.134145 * square)

    def backward_pass(j):
        g, rows = take(gat_g, psem_g, prec_g, j, grad_rows)
        inner = jnp.zeros((unit, 1), F32)
        for t in range(H // tile):
            col = pl.ds(t * tile, tile)
            back = dot(xg[rows, :], wout[col, :], 1, 1)
            low = (back * slope_s[rows, col]).astype(BF)
            bp_s[rows, col] = low
            inner = inner + jnp.sum(low.astype(F32) * pre_s[rows, col], axis=1, keepdims=True)
        inner_s[rows, :] = inner

        def partial_for(q, out):
            weights = win[pl.ds(pl.multiple_of(q * F, 16), F), :]
            blocks = dot(bp_s[rows, :], weights, 1, 1).reshape(ge, M, cap, F)
            joined = jnp.concatenate([blocks[:, m] for m in range(M)], axis=-1)
            out[q, pl.ds(g * ge, ge)] = joined.astype(BF)

        for k in range(PN - 1, 0, -1):
            q = lax.rem(mp + k, PN)
            partial_for(q, rs_s)
            r_copy(q, mp, g).start()

        def inner_row(i):
            e = g * ge + i
            row = as_row(inner_s[pl.ds(pl.multiple_of(e * B, 16), B), :])
            s_s[e] = row
            s_r[mp, e] = row

        repeat(ge, inner_row)
        for k in range(1, PN):
            s_copy(lax.rem(mp + k, PN), mp, g).start()
        partial_for(mp, rs_r)

    def first_grad():
        for t in range(H // tile):
            col = pl.ds(t * tile, tile)
            gin[:, col] = dot(xn[...], bp_s[:, col], 0, 0).astype(BF)
        put_in.start()

    def second_grad():
        for t in range(H // tile):
            col = pl.ds(t * tile, tile)
            gout[col, :] = dot(hid_s[:, col], xg[...], 0, 0).astype(BF)
        put_out.start()

    def t_copy(d, src):
        return pltpu.make_async_remote_copy(
            src_ref=ret_s.at[d], dst_ref=ret_r.at[src], send_sem=tsem.at[d], recv_sem=trec.at[src],
            device_id={"expert": d}, device_id_type=MESH)

    def give_back(j):
        g = lax.rem(mg + groups - j, groups)
        for k in range(1, PN):
            q = lax.rem(mp + k, PN)
            r_copy(q, q, g).wait_recv()
            s_copy(q, q, g).wait_recv()

        def block(i):
            e = g * ge + i
            total = rs_r[0, e].astype(F32)
            inner = s_r[0, e]
            for q in range(1, PN):
                total = total + rs_r[q, e].astype(F32)
                inner = inner + s_r[q, e]
            inner = as_column(inner)
            own = gat_a[mp, e].astype(F32)
            pieces = []
            for m in range(M):
                scale = inv_s[pl.ds(pl.multiple_of(e * B + m * cap, 16), cap), :]
                lanes = slice(m * F, (m + 1) * F)
                factor = scale * scale * inner[m * cap:(m + 1) * cap] / D
                pieces.append(scale * total[:, lanes] - factor * own[:, lanes])
            ret_s[e] = jnp.concatenate(pieces, axis=1).astype(BF)

            @pl.when(e != me)
            def _():
                t_copy(e, me).start()

        repeat(ge, block)

    def up_copy():
        return pltpu.make_async_remote_copy(
            src_ref=grads.at[0], dst_ref=up_r, send_sem=upsem, recv_sem=uprec,
            device_id={"segment": 1 - seg}, device_id_type=MESH)

    def cycle(step):
        lax.fori_loop(0, groups, lambda j, c: (step(j), c)[1], 0)

    put_in = pltpu.make_async_copy(gin, gin_h.at[0, 0], lsem.at[2])
    put_out = pltpu.make_async_copy(gout, gout_h.at[0, 0], lsem.at[3])
    tile = 256 if H % 256 == 0 else 128
    pack([acts[seg, m] for m in range(M)], zs_a)
    for m in range(M):
        gate_s[m] = as_column(gates[seg, pl.ds(m, 1), :])
    pl.semaphore_wait(barrier, E - 1 + PN - 1 + 1)

    @pl.when(seg == 0)
    def _():
        pl.semaphore_wait(go_sem.at[0], 1)

    send_z(zs_a, gat_a, zsem_a, zrec_a)

    @pl.when(seg == 1)
    def _():
        up_r[...] = cot[...]
        send_grad()

    @pl.when(seg == 0)
    def _():
        pl.semaphore_wait(go_sem.at[1], 1)

    def both(j):
        forward(*a_set, j)

        @pl.when(seg == 1)
        def _():
            forward(*g_set, j)

    repeat(groups, both)

    @pl.when(seg == 1)
    def _():
        go(0)

    load_in.wait()
    load_out.wait()
    cycle(forward_pass)

    @pl.when(seg == 0)
    def _():
        up_copy().wait_recv()
        send_grad()
        repeat(groups, lambda j: forward(*g_set, j))

    cycle(backward_pass)

    @pl.when(seg == 0)
    def _():
        first_grad()

    cycle(give_back)
    ret_r[me] = ret_s[me]

    @pl.when(seg == 1)
    def _():
        go(1)

    @pl.when(seg == 0)
    def _():
        second_grad()

    def back_arrive(k):
        src = lax.rem(me + k + 1, E)
        t_copy(src, src).wait_recv()

    repeat(E - 1, back_arrive)
    returned = ret_r[...].reshape(R, M * F)
    for m in range(M):
        restored = dot(placing[m], returned[:, m * F:(m + 1) * F], 0, 0)
        grads[0, m] = (up_r[m].astype(F32) + restored).astype(BF)

    @pl.when(seg == 1)
    def _():
        up_copy().start()
        first_grad()
        second_grad()

    finish(*a_set)
    finish(*g_set)
    for k in range(1, PN):
        q = lax.rem(mp + k, PN)

        def sent(g):
            s_copy(q, mp, g).wait_send()
            r_copy(q, mp, g).wait_send()

        repeat(groups, sent)
    repeat(E - 1, lambda k: t_copy(lax.rem(me + k + 1, E), me).wait_send())
    put_in.wait()
    put_out.wait()

    @pl.when(seg == 1)
    def _():
        up_copy().wait_send()


def place_kernel(a, b, c, a_out, b_out, c_out, sem):
    copies = [pltpu.make_async_copy(a, a_out, sem.at[0])]
    step = b.shape[2] // 4
    for n, (src, dst) in enumerate(((b, b_out), (c, c_out))):
        for i in range(4):
            rows = pl.ds(i * step, step)
            copies.append(pltpu.make_async_copy(src.at[:, :, rows], dst.at[:, :, rows], sem.at[1 + 4 * n + i]))
    for copy in copies:
        copy.start()
    for copy in copies:
        copy.wait()


def body(acts, cotangent, gates, owners, slots, w_in, w_out):
    E = lax.axis_size("expert")
    PN = lax.axis_size("pair")
    M, T, F = cotangent.shape
    D, H = w_in.shape[2:]
    capacity = max(2, (5 * T + 4 * E - 1) // (4 * E))
    cap = (capacity + 15) // 16 * 16
    R = E * cap
    W = M * F
    groups = min(E, 4)
    vm = pltpu.VMEM
    dma = pltpu.SemaphoreType.DMA
    scratch = [
        vm((D, H), BF), vm((H, D), BF), vm((D, H), BF), vm((H, D), BF),
        vm((M, R, T), BF), vm((E, cap, W), BF), vm((E, cap, W), BF),
        vm((PN, E, cap, W), BF), vm((PN, E, cap, W), BF),
        vm((M * R, D), BF), vm((M * R, D), BF), vm((M * R, 1), F32),
        vm((M * R, H), F32), vm((M * R, H), F32), vm((M * R, H), BF), vm((M * R, H), BF),
        vm((E, 1, M * cap), F32), vm((PN, E, 1, M * cap), F32),
        vm((PN, E, cap, W), BF), vm((PN, E, cap, W), BF),
        vm((E, cap, W), BF), vm((E, cap, W), BF), vm((M, T, F), BF),
        vm((M, T, 1), F32), vm((M * R, 1), F32),
        dma((E,)), dma((E,)), dma((E,)), dma((E,)),
        dma((PN, groups)), dma((PN, groups)), dma((PN, groups)), dma((PN, groups)),
        dma((PN, groups)), dma((PN, groups)), dma((PN, groups)), dma((PN, groups)),
        dma((E,)), dma((E,)), dma(()), dma(()), dma((4,)), pltpu.SemaphoreType.REGULAR((2,)),
    ]
    whole = pl.BlockSpec(memory_space=pltpu.VMEM)
    away = pl.BlockSpec(memory_space=pl.ANY)
    shapes = (
            jax.ShapeDtypeStruct((1, M, T, F), BF),
            jax.ShapeDtypeStruct((1, 1, D, H), BF),
            jax.ShapeDtypeStruct((1, 1, H, D), BF),
    )
    held = pl.pallas_call(
        functools.partial(kernel, E, PN, cap),
        out_shape=shapes,
        in_specs=[whole] * 5 + [away] * 2,
        out_specs=(whole, away, away),
        scratch_shapes=scratch,
        compiler_params=pltpu.CompilerParams(
            collective_id=0, has_side_effects=True, vmem_limit_bytes=56 * 1024 * 1024),
        cost_estimate=pl.CostEstimate(
            flops=10 * M * R * D * H, bytes_accessed=8 * D * H, transcendentals=M * R * H),
    )(acts, cotangent, gates, owners, slots, w_in, w_out)
    return pl.pallas_call(
        place_kernel,
        out_shape=shapes,
        in_specs=[pl.BlockSpec(memory_space=pltpu.HBM)] * 3,
        out_specs=(pl.BlockSpec(memory_space=pltpu.HBM),) * 3,
        scratch_shapes=[dma((9,))],
        cost_estimate=pl.CostEstimate(flops=0, bytes_accessed=8 * D * H, transcendentals=0),
    )(*held)


def solution(mesh):
    placed = (
        P(None, None, "expert", "pair"),
        P(None, "expert", "pair"),
        P(None, None, "expert"),
        P(None, None, "expert"),
        P(None, None, "expert"),
        P("segment", "expert", None, "pair"),
        P("segment", "expert", "pair", None),
    )
    return jax.shard_map(
        body,
        mesh=mesh,
        in_specs=placed,
        out_specs=(
            P("segment", None, "expert", "pair"),
            P("segment", "expert", None, "pair"),
            P("segment", "expert", "pair", None),
        ),
        check_vma=False,
    )
```

```python
import functools

import jax
import jax.numpy as jnp
from jax import lax
from jax.experimental import pallas as pl
from jax.experimental.pallas import tpu as pltpu
from jax.sharding import PartitionSpec as P

BF = jnp.bfloat16
F32 = jnp.float32
MESH = pl.DeviceIdType.MESH


def repeat(count, step):
    if count <= 4:
        for i in range(count):
            step(i)
    else:
        lax.fori_loop(0, count, lambda i, c: (step(i), c)[1], 0)


def dot(a, b, ca, cb):
    return lax.dot_general(a, b, (((ca,), (cb,)), ((), ())), preferred_element_type=F32)


def eye(n):
    return lax.broadcasted_iota(jnp.int32, (n, n), 0) == lax.broadcasted_iota(jnp.int32, (n, n), 1)


def as_column(row):
    return jnp.sum(jnp.where(eye(row.shape[1]), row, 0.0), axis=1, keepdims=True)


def as_row(column):
    return jnp.sum(jnp.where(eye(column.shape[0]), column, 0.0), axis=0, keepdims=True)


def kernel(
    E, PN, cap, acts, cot, gates, owners, slots, win_h, wout_h, grads, gin_h, gout_h,
    win, wout, gin, gout, placing, zs_a, zs_g, gat_a, gat_g, xn, xg, inv_s, pre_s, slope_s, hid_s, bp_s,
    s_s, s_r, rs_s, rs_r, ret_s, ret_r, up_r, gate_s, inner_s, xn_t, hid_t, placing_t,
    zsem_a, zrec_a, zsem_g, zrec_g, psem_a, prec_a, psem_g, prec_g,
    ssem, srec, rsem, rrec, tsem, trec, upsem, uprec, lsem, go_sem,
):
    seg = lax.axis_index("segment")
    me = lax.axis_index("expert")
    mp = lax.axis_index("pair")
    M, T, F = cot.shape
    D = F * PN
    H = win.shape[1]
    R = E * cap
    B = M * cap
    groups = min(E, 4)
    ge = E // groups
    mg = me // ge

    load_in = pltpu.make_async_copy(win_h.at[0, 0], win, lsem.at[0])
    load_out = pltpu.make_async_copy(wout_h.at[0, 0], wout, lsem.at[1])
    load_in.start()
    load_out.start()

    barrier = pltpu.get_barrier_semaphore()

    def greet_e(k):
        pl.semaphore_signal(barrier, inc=1, device_id={"expert": lax.rem(me + k + 1, E)}, device_id_type=MESH)

    repeat(E - 1, greet_e)
    for k in range(1, PN):
        pl.semaphore_signal(barrier, inc=1, device_id={"pair": lax.rem(mp + k, PN)}, device_id_type=MESH)
    pl.semaphore_signal(barrier, inc=1, device_id={"segment": 1 - seg}, device_id_type=MESH)

    for m in range(M):
        target = owners[seg, pl.ds(m, 1), :] * cap + slots[seg, pl.ds(m, 1), :]
        placing[m] = (lax.broadcasted_iota(jnp.int32, (R, T), 0) == target).astype(BF)

    def pack(values, zs):
        rows = [dot(placing[m], values[m], 1, 0) for m in range(M)]
        zs[...] = jnp.concatenate(rows, axis=1).astype(BF).reshape(E, cap, M * F)

    def z_copy(zs, gat, ssems, rsems, d, src):
        return pltpu.make_async_remote_copy(
            src_ref=zs.at[d], dst_ref=gat.at[mp, src], send_sem=ssems.at[d], recv_sem=rsems.at[src],
            device_id={"expert": d}, device_id_type=MESH)

    def send_z(zs, gat, ssems, rsems):
        repeat(E - 1, lambda k: z_copy(zs, gat, ssems, rsems, lax.rem(me + k + 1, E), me).start())
        gat[mp, me] = zs[me]

    def p_copy(gat, ssems, rsems, q, src, g):
        part = gat.at[src, pl.ds(g * ge, ge)]
        return pltpu.make_async_remote_copy(
            src_ref=part, dst_ref=part, send_sem=ssems.at[q, g], recv_sem=rsems.at[src, g],
            device_id={"pair": q}, device_id_type=MESH)

    def forward(zs, gat, zsems, zrecs, psems, precs, j):
        g = lax.rem(mg + groups - j, groups)

        def arrive(i):
            e = g * ge + i

            @pl.when(e != me)
            def _():
                z_copy(zs, gat, zsems, zrecs, e, e).wait_recv()

        repeat(ge, arrive)
        for k in range(PN - 1, 0, -1):
            p_copy(gat, psems, precs, lax.rem(mp + k, PN), mp, g).start()

    def gathered(gat, psems, precs, j):
        g = lax.rem(mg + groups - j, groups)
        for k in range(1, PN):
            q = lax.rem(mp + k, PN)
            p_copy(gat, psems, precs, q, q, g).wait_recv()
        return g

    def finish(zs, gat, zsems, zrecs, psems, precs):
        repeat(E - 1, lambda k: z_copy(zs, gat, zsems, zrecs, lax.rem(me + k + 1, E), me).wait_send())

        def one(g):
            for k in range(1, PN):
                p_copy(gat, psems, precs, lax.rem(mp + k, PN), mp, g).wait_send()

        repeat(groups, one)

    a_set = (zs_a, gat_a, zsem_a, zrec_a, psem_a, prec_a)
    g_set = (zs_g, gat_g, zsem_g, zrec_g, psem_g, prec_g)
    unit = ge * B

    def go(i):
        pl.semaphore_signal(go_sem.at[i], inc=1, device_id={"segment": 1 - seg}, device_id_type=MESH)

    def send_grad():
        scaled = [(gate_s[m] * up_r[m].astype(F32)).astype(BF) for m in range(M)]
        pack(scaled, zs_g)
        send_z(zs_g, gat_g, zsem_g, zrec_g)

    def take(gat, psems, precs, j, use):
        g = gathered(gat, psems, precs, j)

        def block(i):
            e = g * ge + i
            parts = [gat[q, e].astype(F32) for q in range(PN)]
            for m in range(M):
                full = jnp.concatenate([v[:, m * F:(m + 1) * F] for v in parts], axis=1)
                use(pl.ds(pl.multiple_of(e * B + m * cap, 16), cap), full)

        repeat(ge, block)
        return g, pl.ds(pl.multiple_of(g * unit, 16), unit)

    def norm_rows(rows, full):
        scale = lax.rsqrt(jnp.mean(full * full, axis=1, keepdims=True) + 1e-06)
        inv_s[rows, :] = scale
        xn[rows, :] = (full * scale).astype(BF)

    def grad_rows(rows, full):
        xg[rows, :] = full.astype(BF)

    def r_copy(q, src, g):
        rows = pl.ds(g * ge, ge)
        return pltpu.make_async_remote_copy(
            src_ref=rs_s.at[q, rows], dst_ref=rs_r.at[src, rows], send_sem=rsem.at[q, g], recv_sem=rrec.at[src, g],
            device_id={"pair": q}, device_id_type=MESH)

    def s_copy(q, src, g):
        rows = pl.ds(g * ge, ge)
        return pltpu.make_async_remote_copy(
            src_ref=s_s.at[rows], dst_ref=s_r.at[src, rows], send_sem=ssem.at[q, g], recv_sem=srec.at[src, g],
            device_id={"pair": q}, device_id_type=MESH)

    def forward_pass(j):
        _, rows = take(gat_a, psem_a, prec_a, j, norm_rows)
        for t in range(H // tile):
            col = pl.ds(t * tile, tile)
            u = dot(xn[rows, :], win[:, col], 1, 0)
            square = u * u
            tangent = jnp.tanh(0.7978845608 * (u + 0.044715 * square * u))
            pre_s[rows, col] = u
            hid_s[rows, col] = (0.5 * u * (1.0 + tangent)).astype(BF)
            slope_s[rows, col] = 0.5 * (1.0 + tangent) + 0.5 * u * (1.0 - tangent * tangent) * 0.7978845608 * (
                1.0 + 0.134145 * square)

    def backward_pass(j):
        g, rows = take(gat_g, psem_g, prec_g, j, grad_rows)
        inner = jnp.zeros((unit, 1), F32)
        for t in range(H // tile):
            col = pl.ds(t * tile, tile)
            back = dot(xg[rows, :], wout[col, :], 1, 1)
            low = (back * slope_s[rows, col]).astype(BF)
            bp_s[rows, col] = low
            inner = inner + jnp.sum(low.astype(F32) * pre_s[rows, col], axis=1, keepdims=True)
        inner_s[rows, :] = inner

        def partial_for(q, out):
            weights = win[pl.ds(pl.multiple_of(q * F, 16), F), :]
            blocks = dot(bp_s[rows, :], weights, 1, 1).reshape(ge, M, cap, F)
            joined = jnp.concatenate([blocks[:, m] for m in range(M)], axis=-1)
            out[q, pl.ds(g * ge, ge)] = joined.astype(BF)

        for k in range(PN - 1, 0, -1):
            q = lax.rem(mp + k, PN)
            partial_for(q, rs_s)
            r_copy(q, mp, g).start()

        def inner_row(i):
            e = g * ge + i
            row = as_row(inner_s[pl.ds(pl.multiple_of(e * B, 16), B), :])
            s_s[e] = row
            s_r[mp, e] = row

        repeat(ge, inner_row)
        for k in range(1, PN):
            s_copy(lax.rem(mp + k, PN), mp, g).start()
        partial_for(mp, rs_r)

    def turn():
        for t in range(D // 128):
            xn_t[pl.ds(t * 128, 128), :] = jnp.transpose(xn[:, pl.ds(t * 128, 128)])
        for t in range(H // 128):
            hid_t[pl.ds(t * 128, 128), :] = jnp.transpose(hid_s[:, pl.ds(t * 128, 128)])

    def first_grad():
        for t in range(H // tile):
            col = pl.ds(t * tile, tile)
            gin[:, col] = dot(xn_t[...], bp_s[:, col], 1, 0).astype(BF)
        put_in.start()

    def second_grad():
        for t in range(H // tile):
            col = pl.ds(t * tile, tile)
            gout[col, :] = dot(hid_t[col, :], xg[...], 1, 0).astype(BF)
        put_out.start()

    def t_copy(d, src):
        return pltpu.make_async_remote_copy(
            src_ref=ret_s.at[d], dst_ref=ret_r.at[src], send_sem=tsem.at[d], recv_sem=trec.at[src],
            device_id={"expert": d}, device_id_type=MESH)

    def give_back(j):
        g = lax.rem(mg + groups - j, groups)
        for k in range(1, PN):
            q = lax.rem(mp + k, PN)
            r_copy(q, q, g).wait_recv()
            s_copy(q, q, g).wait_recv()

        def block(i):
            e = g * ge + i
            total = rs_r[0, e].astype(F32)
            inner = s_r[0, e]
            for q in range(1, PN):
                total = total + rs_r[q, e].astype(F32)
                inner = inner + s_r[q, e]
            inner = as_column(inner)
            own = gat_a[mp, e].astype(F32)
            pieces = []
            for m in range(M):
                scale = inv_s[pl.ds(pl.multiple_of(e * B + m * cap, 16), cap), :]
                lanes = slice(m * F, (m + 1) * F)
                factor = scale * scale * inner[m * cap:(m + 1) * cap] / D
                pieces.append(scale * total[:, lanes] - factor * own[:, lanes])
            ret_s[e] = jnp.concatenate(pieces, axis=1).astype(BF)

            @pl.when(e != me)
            def _():
                t_copy(e, me).start()

        repeat(ge, block)

    def up_copy():
        return pltpu.make_async_remote_copy(
            src_ref=grads.at[0], dst_ref=up_r, send_sem=upsem, recv_sem=uprec,
            device_id={"segment": 1 - seg}, device_id_type=MESH)

    def cycle(step):
        lax.fori_loop(0, groups, lambda j, c: (step(j), c)[1], 0)

    put_in = pltpu.make_async_copy(gin, gin_h.at[0, 0], lsem.at[2])
    put_out = pltpu.make_async_copy(gout, gout_h.at[0, 0], lsem.at[3])
    tile = 256 if H % 256 == 0 else 128
    pack([acts[seg, m] for m in range(M)], zs_a)
    for m in range(M):
        gate_s[m] = as_column(gates[seg, pl.ds(m, 1), :])
        spot = owners[seg, pl.ds(m, 1), :] * cap + slots[seg, pl.ds(m, 1), :]
        spot = as_column(spot.astype(F32)).astype(jnp.int32)
        placing_t[m] = (lax.broadcasted_iota(jnp.int32, (T, R), 1) == spot).astype(BF)
    pl.semaphore_wait(barrier, E - 1 + PN - 1 + 1)

    @pl.when(seg == 0)
    def _():
        pl.semaphore_wait(go_sem.at[0], 1)

    send_z(zs_a, gat_a, zsem_a, zrec_a)

    @pl.when(seg == 1)
    def _():
        up_r[...] = cot[...]
        send_grad()

    @pl.when(seg == 0)
    def _():
        pl.semaphore_wait(go_sem.at[1], 1)

    def both(j):
        forward(*a_set, j)

        @pl.when(seg == 1)
        def _():
            forward(*g_set, j)

    repeat(groups, both)

    @pl.when(seg == 1)
    def _():
        go(0)

    load_in.wait()
    load_out.wait()
    cycle(forward_pass)

    @pl.when(seg == 0)
    def _():
        turn()
        up_copy().wait_recv()
        send_grad()
        repeat(groups, lambda j: forward(*g_set, j))

    cycle(backward_pass)

    @pl.when(seg == 1)
    def _():
        go(1)

    @pl.when(seg == 0)
    def _():
        first_grad()

    cycle(give_back)
    ret_r[me] = ret_s[me]

    @pl.when(seg == 0)
    def _():
        second_grad()

    def back_arrive(k):
        src = lax.rem(me + k + 1, E)
        t_copy(src, src).wait_recv()

    repeat(E - 1, back_arrive)
    returned = ret_r[...].reshape(R, M * F)
    for m in range(M):
        restored = dot(placing_t[m], returned[:, m * F:(m + 1) * F], 1, 0)
        grads[0, m] = (up_r[m].astype(F32) + restored).astype(BF)

    @pl.when(seg == 1)
    def _():
        up_copy().start()
        turn()
        first_grad()
        second_grad()

    finish(*a_set)
    finish(*g_set)
    for k in range(1, PN):
        q = lax.rem(mp + k, PN)

        def sent(g):
            s_copy(q, mp, g).wait_send()
            r_copy(q, mp, g).wait_send()

        repeat(groups, sent)
    repeat(E - 1, lambda k: t_copy(lax.rem(me + k + 1, E), me).wait_send())
    put_in.wait()
    put_out.wait()

    @pl.when(seg == 1)
    def _():
        up_copy().wait_send()


def place_kernel(a, b, c, a_out, b_out, c_out):
    a_out[...] = a[...]
    b_out[...] = b[...]
    c_out[...] = c[...]


def body(acts, cotangent, gates, owners, slots, w_in, w_out):
    E = lax.axis_size("expert")
    PN = lax.axis_size("pair")
    M, T, F = cotangent.shape
    D, H = w_in.shape[2:]
    capacity = max(2, (5 * T + 4 * E - 1) // (4 * E))
    cap = (capacity + 15) // 16 * 16
    R = E * cap
    W = M * F
    groups = min(E, 4)
    vm = pltpu.VMEM
    dma = pltpu.SemaphoreType.DMA
    scratch = [
        vm((D, H), BF), vm((H, D), BF), vm((D, H), BF), vm((H, D), BF),
        vm((M, R, T), BF), vm((E, cap, W), BF), vm((E, cap, W), BF),
        vm((PN, E, cap, W), BF), vm((PN, E, cap, W), BF),
        vm((M * R, D), BF), vm((M * R, D), BF), vm((M * R, 1), F32),
        vm((M * R, H), F32), vm((M * R, H), F32), vm((M * R, H), BF), vm((M * R, H), BF),
        vm((E, 1, M * cap), F32), vm((PN, E, 1, M * cap), F32),
        vm((PN, E, cap, W), BF), vm((PN, E, cap, W), BF),
        vm((E, cap, W), BF), vm((E, cap, W), BF), vm((M, T, F), BF),
        vm((M, T, 1), F32), vm((M * R, 1), F32),
        vm((D, M * R), BF), vm((H, M * R), BF), vm((M, T, R), BF),
        dma((E,)), dma((E,)), dma((E,)), dma((E,)),
        dma((PN, groups)), dma((PN, groups)), dma((PN, groups)), dma((PN, groups)),
        dma((PN, groups)), dma((PN, groups)), dma((PN, groups)), dma((PN, groups)),
        dma((E,)), dma((E,)), dma(()), dma(()), dma((4,)), pltpu.SemaphoreType.REGULAR((2,)),
    ]
    whole = pl.BlockSpec(memory_space=pltpu.VMEM)
    away = pl.BlockSpec(memory_space=pl.ANY)
    shapes = (
            jax.ShapeDtypeStruct((1, M, T, F), BF),
            jax.ShapeDtypeStruct((1, 1, D, H), BF),
            jax.ShapeDtypeStruct((1, 1, H, D), BF),
    )
    held = pl.pallas_call(
        functools.partial(kernel, E, PN, cap),
        out_shape=shapes,
        in_specs=[whole] * 5 + [away] * 2,
        out_specs=(whole, away, away),
        scratch_shapes=scratch,
        compiler_params=pltpu.CompilerParams(
            collective_id=0, has_side_effects=True, vmem_limit_bytes=56 * 1024 * 1024),
        cost_estimate=pl.CostEstimate(
            flops=10 * M * R * D * H, bytes_accessed=8 * D * H, transcendentals=M * R * H),
    )(acts, cotangent, gates, owners, slots, w_in, w_out)
    steps = 4
    slices = [
        pl.BlockSpec((1, M, T // steps, F), lambda i: (0, 0, i, 0)),
        pl.BlockSpec((1, 1, D // steps, H), lambda i: (0, 0, i, 0)),
        pl.BlockSpec((1, 1, H // steps, D), lambda i: (0, 0, i, 0)),
    ]
    return pl.pallas_call(
        place_kernel,
        grid=(steps,),
        out_shape=shapes,
        in_specs=slices,
        out_specs=tuple(slices),
        cost_estimate=pl.CostEstimate(flops=0, bytes_accessed=8 * D * H, transcendentals=0),
    )(*held)


def solution(mesh):
    placed = (
        P(None, None, "expert", "pair"),
        P(None, "expert", "pair"),
        P(None, None, "expert"),
        P(None, None, "expert"),
        P(None, None, "expert"),
        P("segment", "expert", None, "pair"),
        P("segment", "expert", "pair", None),
    )
    return jax.shard_map(
        body,
        mesh=mesh,
        in_specs=placed,
        out_specs=(
            P("segment", None, "expert", "pair"),
            P("segment", "expert", None, "pair"),
            P("segment", "expert", "pair", None),
        ),
        check_vma=False,
    )
```

```python
import functools

import jax
import jax.numpy as jnp
from jax import lax
from jax.experimental import pallas as pl
from jax.experimental.pallas import tpu as pltpu
from jax.sharding import PartitionSpec as P

BF = jnp.bfloat16
F32 = jnp.float32
MESH = pl.DeviceIdType.MESH


def repeat(count, step):
    if count <= 4:
        for i in range(count):
            step(i)
    else:
        lax.fori_loop(0, count, lambda i, c: (step(i), c)[1], 0)


def dot(a, b, ca, cb):
    return lax.dot_general(a, b, (((ca,), (cb,)), ((), ())), preferred_element_type=F32)


def eye(n):
    return lax.broadcasted_iota(jnp.int32, (n, n), 0) == lax.broadcasted_iota(jnp.int32, (n, n), 1)


def as_column(row):
    return jnp.sum(jnp.where(eye(row.shape[1]), row, 0.0), axis=1, keepdims=True)


def as_row(column):
    return jnp.sum(jnp.where(eye(column.shape[0]), column, 0.0), axis=0, keepdims=True)


def kernel(
    E, PN, cap, acts, cot, gates, owners, slots, win_h, wout_h, grads, gin_h, gout_h,
    win, wout, gin, gout, placing, zs_a, zs_g, gat_a, gat_g, xn, xg, inv_s, pre_s, slope_s, hid_s, bp_s,
    s_s, s_r, rs_s, rs_r, ret_s, ret_r, up_r, gate_s, inner_s, xn_t, hid_t, placing_t, win_t, wout_t,
    zsem_a, zrec_a, zsem_g, zrec_g, psem_a, prec_a, psem_g, prec_g,
    ssem, srec, rsem, rrec, tsem, trec, upsem, uprec, lsem, go_sem,
):
    seg = lax.axis_index("segment")
    me = lax.axis_index("expert")
    mp = lax.axis_index("pair")
    M, T, F = cot.shape
    D = F * PN
    H = win.shape[1]
    R = E * cap
    B = M * cap
    groups = min(E, 4)
    ge = E // groups
    mg = me // ge

    load_in = pltpu.make_async_copy(win_h.at[0, 0], win, lsem.at[0])
    load_out = pltpu.make_async_copy(wout_h.at[0, 0], wout, lsem.at[1])
    load_in.start()
    load_out.start()

    barrier = pltpu.get_barrier_semaphore()

    def greet_e(k):
        pl.semaphore_signal(barrier, inc=1, device_id={"expert": lax.rem(me + k + 1, E)}, device_id_type=MESH)

    repeat(E - 1, greet_e)
    for k in range(1, PN):
        pl.semaphore_signal(barrier, inc=1, device_id={"pair": lax.rem(mp + k, PN)}, device_id_type=MESH)
    pl.semaphore_signal(barrier, inc=1, device_id={"segment": 1 - seg}, device_id_type=MESH)

    for m in range(M):
        target = owners[seg, pl.ds(m, 1), :] * cap + slots[seg, pl.ds(m, 1), :]
        placing[m] = (lax.broadcasted_iota(jnp.int32, (R, T), 0) == target).astype(BF)

    def pack(values, zs):
        rows = [dot(placing[m], values[m], 1, 0) for m in range(M)]
        zs[...] = jnp.concatenate(rows, axis=1).astype(BF).reshape(E, cap, M * F)

    def z_copy(zs, gat, ssems, rsems, d, src):
        return pltpu.make_async_remote_copy(
            src_ref=zs.at[d], dst_ref=gat.at[mp, src], send_sem=ssems.at[d], recv_sem=rsems.at[src],
            device_id={"expert": d}, device_id_type=MESH)

    def send_z(zs, gat, ssems, rsems):
        repeat(E - 1, lambda k: z_copy(zs, gat, ssems, rsems, lax.rem(me + k + 1, E), me).start())
        gat[mp, me] = zs[me]

    def p_copy(gat, ssems, rsems, q, src, g):
        part = gat.at[src, pl.ds(g * ge, ge)]
        return pltpu.make_async_remote_copy(
            src_ref=part, dst_ref=part, send_sem=ssems.at[q, g], recv_sem=rsems.at[src, g],
            device_id={"pair": q}, device_id_type=MESH)

    def forward(zs, gat, zsems, zrecs, psems, precs, j):
        g = lax.rem(mg + groups - j, groups)

        def arrive(i):
            e = g * ge + i

            @pl.when(e != me)
            def _():
                z_copy(zs, gat, zsems, zrecs, e, e).wait_recv()

        repeat(ge, arrive)
        for k in range(PN - 1, 0, -1):
            p_copy(gat, psems, precs, lax.rem(mp + k, PN), mp, g).start()

    def gathered(gat, psems, precs, j):
        g = lax.rem(mg + groups - j, groups)
        for k in range(1, PN):
            q = lax.rem(mp + k, PN)
            p_copy(gat, psems, precs, q, q, g).wait_recv()
        return g

    def finish(zs, gat, zsems, zrecs, psems, precs):
        repeat(E - 1, lambda k: z_copy(zs, gat, zsems, zrecs, lax.rem(me + k + 1, E), me).wait_send())

        def one(g):
            for k in range(1, PN):
                p_copy(gat, psems, precs, lax.rem(mp + k, PN), mp, g).wait_send()

        repeat(groups, one)

    a_set = (zs_a, gat_a, zsem_a, zrec_a, psem_a, prec_a)
    g_set = (zs_g, gat_g, zsem_g, zrec_g, psem_g, prec_g)
    unit = ge * B

    def go(i):
        pl.semaphore_signal(go_sem.at[i], inc=1, device_id={"segment": 1 - seg}, device_id_type=MESH)

    def send_grad():
        scaled = [(gate_s[m] * up_r[m].astype(F32)).astype(BF) for m in range(M)]
        pack(scaled, zs_g)
        send_z(zs_g, gat_g, zsem_g, zrec_g)

    def take(gat, psems, precs, j, use):
        g = gathered(gat, psems, precs, j)

        def block(i):
            e = g * ge + i
            parts = [gat[q, e].astype(F32) for q in range(PN)]
            for m in range(M):
                full = jnp.concatenate([v[:, m * F:(m + 1) * F] for v in parts], axis=1)
                use(pl.ds(pl.multiple_of(e * B + m * cap, 16), cap), full)

        repeat(ge, block)
        return g, pl.ds(pl.multiple_of(g * unit, 16), unit)

    def norm_rows(rows, full):
        scale = lax.rsqrt(jnp.mean(full * full, axis=1, keepdims=True) + 1e-06)
        inv_s[rows, :] = scale
        xn[rows, :] = (full * scale).astype(BF)

    def grad_rows(rows, full):
        xg[rows, :] = full.astype(BF)

    def r_copy(q, src, g):
        rows = pl.ds(g * ge, ge)
        return pltpu.make_async_remote_copy(
            src_ref=rs_s.at[q, rows], dst_ref=rs_r.at[src, rows], send_sem=rsem.at[q, g], recv_sem=rrec.at[src, g],
            device_id={"pair": q}, device_id_type=MESH)

    def s_copy(q, src, g):
        rows = pl.ds(g * ge, ge)
        return pltpu.make_async_remote_copy(
            src_ref=s_s.at[rows], dst_ref=s_r.at[src, rows], send_sem=ssem.at[q, g], recv_sem=srec.at[src, g],
            device_id={"pair": q}, device_id_type=MESH)

    def forward_pass(j):
        _, rows = take(gat_a, psem_a, prec_a, j, norm_rows)
        for t in range(H // tile):
            col = pl.ds(t * tile, tile)
            u = dot(xn[rows, :], win[:, col], 1, 0)
            square = u * u
            tangent = jnp.tanh(0.7978845608 * (u + 0.044715 * square * u))
            pre_s[rows, col] = u.astype(BF)
            hid_s[rows, col] = (0.5 * u * (1.0 + tangent)).astype(BF)
            slope_s[rows, col] = 0.5 * (1.0 + tangent) + 0.5 * u * (1.0 - tangent * tangent) * 0.7978845608 * (
                1.0 + 0.134145 * square)

    def backward_pass(j):
        g, rows = take(gat_g, psem_g, prec_g, j, grad_rows)
        inner = jnp.zeros((unit, tile), F32)
        for t in range(H // tile):
            col = pl.ds(t * tile, tile)
            back = dot(xg[rows, :], wout_t[:, col], 1, 0)
            low = (back * slope_s[rows, col]).astype(BF)
            bp_s[rows, col] = low
            inner = inner + low.astype(F32) * pre_s[rows, col].astype(F32)
        inner_s[rows, :] = jnp.sum(inner, axis=1, keepdims=True)
        part = dot(bp_s[rows, :], win_t[...], 1, 0).reshape(ge, M, cap, D)
        for q in range(PN):
            joined = jnp.concatenate([part[:, m, :, q * F:(q + 1) * F] for m in range(M)], axis=-1)
            rs_s[q, pl.ds(g * ge, ge)] = joined.astype(BF)
        for k in range(PN - 1, 0, -1):
            r_copy(lax.rem(mp + k, PN), mp, g).start()

        def inner_row(i):
            e = g * ge + i
            row = as_row(inner_s[pl.ds(pl.multiple_of(e * B, 16), B), :])
            s_s[e] = row
            s_r[mp, e] = row

        repeat(ge, inner_row)
        for k in range(1, PN):
            s_copy(lax.rem(mp + k, PN), mp, g).start()
        rs_r[mp, pl.ds(g * ge, ge)] = rs_s[mp, pl.ds(g * ge, ge)]

    def turn():
        for t in range(D // 128):
            xn_t[pl.ds(t * 128, 128), :] = jnp.transpose(xn[:, pl.ds(t * 128, 128)])
        for t in range(H // 128):
            hid_t[pl.ds(t * 128, 128), :] = jnp.transpose(hid_s[:, pl.ds(t * 128, 128)])

    def first_grad():
        for t in range(H // tile):
            col = pl.ds(t * tile, tile)
            gin[:, col] = dot(xn_t[...], bp_s[:, col], 1, 0).astype(BF)
        put_in.start()

    def second_grad():
        for t in range(H // tile):
            col = pl.ds(t * tile, tile)
            gout[col, :] = dot(hid_t[col, :], xg[...], 1, 0).astype(BF)
        put_out.start()

    def t_copy(d, src):
        return pltpu.make_async_remote_copy(
            src_ref=ret_s.at[d], dst_ref=ret_r.at[src], send_sem=tsem.at[d], recv_sem=trec.at[src],
            device_id={"expert": d}, device_id_type=MESH)

    def give_back(j):
        g = lax.rem(mg + groups - j, groups)
        for k in range(1, PN):
            q = lax.rem(mp + k, PN)
            r_copy(q, q, g).wait_recv()
            s_copy(q, q, g).wait_recv()

        def block(i):
            e = g * ge + i
            total = rs_r[0, e].astype(F32)
            inner = s_r[0, e]
            for q in range(1, PN):
                total = total + rs_r[q, e].astype(F32)
                inner = inner + s_r[q, e]
            inner = as_column(inner)
            own = gat_a[mp, e].astype(F32)
            pieces = []
            for m in range(M):
                scale = inv_s[pl.ds(pl.multiple_of(e * B + m * cap, 16), cap), :]
                lanes = slice(m * F, (m + 1) * F)
                factor = scale * scale * inner[m * cap:(m + 1) * cap] / D
                pieces.append(scale * total[:, lanes] - factor * own[:, lanes])
            ret_s[e] = jnp.concatenate(pieces, axis=1).astype(BF)

            @pl.when(e != me)
            def _():
                t_copy(e, me).start()

        repeat(ge, block)

    def up_copy():
        return pltpu.make_async_remote_copy(
            src_ref=grads.at[0], dst_ref=up_r, send_sem=upsem, recv_sem=uprec,
            device_id={"segment": 1 - seg}, device_id_type=MESH)

    def cycle(step):
        lax.fori_loop(0, groups, lambda j, c: (step(j), c)[1], 0)

    put_in = pltpu.make_async_copy(gin, gin_h.at[0, 0], lsem.at[2])
    put_out = pltpu.make_async_copy(gout, gout_h.at[0, 0], lsem.at[3])
    tile = 256 if H % 256 == 0 else 128
    pack([acts[seg, m] for m in range(M)], zs_a)
    for m in range(M):
        gate_s[m] = as_column(gates[seg, pl.ds(m, 1), :])
        spot = owners[seg, pl.ds(m, 1), :] * cap + slots[seg, pl.ds(m, 1), :]
        spot = as_column(spot.astype(F32)).astype(jnp.int32)
        placing_t[m] = (lax.broadcasted_iota(jnp.int32, (T, R), 1) == spot).astype(BF)
    pl.semaphore_wait(barrier, E - 1 + PN - 1 + 1)

    @pl.when(seg == 0)
    def _():
        pl.semaphore_wait(go_sem.at[0], 1)

    send_z(zs_a, gat_a, zsem_a, zrec_a)

    @pl.when(seg == 1)
    def _():
        up_r[...] = cot[...]
        send_grad()

    load_in.wait()
    load_out.wait()
    for t in range(H // 128):
        col = pl.ds(t * 128, 128)
        win_t[col, :] = jnp.transpose(win[:, col])
    for t in range(D // 128):
        col = pl.ds(t * 128, 128)
        wout_t[col, :] = jnp.transpose(wout[:, col])

    @pl.when(seg == 0)
    def _():
        pl.semaphore_wait(go_sem.at[1], 1)

    def both(j):
        forward(*a_set, j)

        @pl.when(seg == 1)
        def _():
            forward(*g_set, j)

    repeat(groups, both)

    @pl.when(seg == 1)
    def _():
        go(0)

    cycle(forward_pass)

    @pl.when(seg == 0)
    def _():
        turn()
        up_copy().wait_recv()
        send_grad()
        repeat(groups, lambda j: forward(*g_set, j))

    cycle(backward_pass)

    @pl.when(seg == 1)
    def _():
        go(1)

    @pl.when(seg == 0)
    def _():
        first_grad()

    cycle(give_back)
    ret_r[me] = ret_s[me]

    @pl.when(seg == 0)
    def _():
        second_grad()

    def back_arrive(k):
        src = lax.rem(me + k + 1, E)
        t_copy(src, src).wait_recv()

    repeat(E - 1, back_arrive)
    returned = ret_r[...].reshape(R, M * F)
    for m in range(M):
        restored = dot(placing_t[m], returned[:, m * F:(m + 1) * F], 1, 0)
        grads[0, m] = (up_r[m].astype(F32) + restored).astype(BF)

    @pl.when(seg == 1)
    def _():
        up_copy().start()
        turn()
        first_grad()
        second_grad()

    finish(*a_set)
    finish(*g_set)
    for k in range(1, PN):
        q = lax.rem(mp + k, PN)

        def sent(g):
            s_copy(q, mp, g).wait_send()
            r_copy(q, mp, g).wait_send()

        repeat(groups, sent)
    repeat(E - 1, lambda k: t_copy(lax.rem(me + k + 1, E), me).wait_send())
    put_in.wait()
    put_out.wait()

    @pl.when(seg == 1)
    def _():
        up_copy().wait_send()


def place_kernel(a, b, c, a_out, b_out, c_out, a_mid, b_mid, c_mid, in_sem, out_sem):
    moves = []
    for src, mid, dst, axis in ((a, a_mid, a_out, 1), (b, b_mid, b_out, 2), (c, c_mid, c_out, 2)):
        cuts = src.shape[1] if axis == 1 else 4
        step = src.shape[axis] // cuts
        for i in range(cuts):
            at = (slice(None),) * axis + (pl.ds(i * step, step),)
            n = len(moves)
            moves.append((
                pltpu.make_async_copy(src.at[at], mid.at[at], in_sem.at[n]),
                pltpu.make_async_copy(mid.at[at], dst.at[at], out_sem.at[n]),
            ))
    for first, _ in moves:
        first.start()
    for first, second in moves:
        first.wait()
        second.start()
    for _, second in moves:
        second.wait()


def body(acts, cotangent, gates, owners, slots, w_in, w_out):
    E = lax.axis_size("expert")
    PN = lax.axis_size("pair")
    M, T, F = cotangent.shape
    D, H = w_in.shape[2:]
    capacity = max(2, (5 * T + 4 * E - 1) // (4 * E))
    cap = (capacity + 15) // 16 * 16
    R = E * cap
    W = M * F
    groups = min(E, 4)
    vm = pltpu.VMEM
    dma = pltpu.SemaphoreType.DMA
    scratch = [
        vm((D, H), BF), vm((H, D), BF), vm((D, H), BF), vm((H, D), BF),
        vm((M, R, T), BF), vm((E, cap, W), BF), vm((E, cap, W), BF),
        vm((PN, E, cap, W), BF), vm((PN, E, cap, W), BF),
        vm((M * R, D), BF), vm((M * R, D), BF), vm((M * R, 1), F32),
        vm((M * R, H), BF), vm((M * R, H), F32), vm((M * R, H), BF), vm((M * R, H), BF),
        vm((E, 1, M * cap), F32), vm((PN, E, 1, M * cap), F32),
        vm((PN, E, cap, W), BF), vm((PN, E, cap, W), BF),
        vm((E, cap, W), BF), vm((E, cap, W), BF), vm((M, T, F), BF),
        vm((M, T, 1), F32), vm((M * R, 1), F32),
        vm((D, M * R), BF), vm((H, M * R), BF), vm((M, T, R), BF), vm((H, D), BF), vm((D, H), BF),
        dma((E,)), dma((E,)), dma((E,)), dma((E,)),
        dma((PN, groups)), dma((PN, groups)), dma((PN, groups)), dma((PN, groups)),
        dma((PN, groups)), dma((PN, groups)), dma((PN, groups)), dma((PN, groups)),
        dma((E,)), dma((E,)), dma(()), dma(()), dma((4,)), pltpu.SemaphoreType.REGULAR((2,)),
    ]
    whole = pl.BlockSpec(memory_space=pltpu.VMEM)
    away = pl.BlockSpec(memory_space=pl.ANY)
    shapes = (
            jax.ShapeDtypeStruct((1, M, T, F), BF),
            jax.ShapeDtypeStruct((1, 1, D, H), BF),
            jax.ShapeDtypeStruct((1, 1, H, D), BF),
    )
    held = pl.pallas_call(
        functools.partial(kernel, E, PN, cap),
        out_shape=shapes,
        in_specs=[whole] * 5 + [away] * 2,
        out_specs=(whole, away, away),
        scratch_shapes=scratch,
        compiler_params=pltpu.CompilerParams(
            collective_id=0, has_side_effects=True, vmem_limit_bytes=58 * 1024 * 1024),
        cost_estimate=pl.CostEstimate(
            flops=10 * M * R * D * H, bytes_accessed=8 * D * H, transcendentals=M * R * H),
    )(acts, cotangent, gates, owners, slots, w_in, w_out)
    return pl.pallas_call(
        place_kernel,
        out_shape=shapes,
        in_specs=[away] * 3,
        out_specs=(away,) * 3,
        scratch_shapes=[vm(x.shape, BF) for x in shapes] + [dma((M + 8,)), dma((M + 8,))],
        cost_estimate=pl.CostEstimate(flops=0, bytes_accessed=8 * D * H, transcendentals=0),
    )(*held)


def solution(mesh):
    placed = (
        P(None, None, "expert", "pair"),
        P(None, "expert", "pair"),
        P(None, None, "expert"),
        P(None, None, "expert"),
        P(None, None, "expert"),
        P("segment", "expert", None, "pair"),
        P("segment", "expert", "pair", None),
    )
    return jax.shard_map(
        body,
        mesh=mesh,
        in_specs=placed,
        out_specs=(
            P("segment", None, "expert", "pair"),
            P("segment", "expert", None, "pair"),
            P("segment", "expert", "pair", None),
        ),
        check_vma=False,
    )
```

```python
import functools

import jax
import jax.numpy as jnp
from jax import lax
from jax.experimental import pallas as pl
from jax.experimental.pallas import tpu as pltpu
from jax.sharding import PartitionSpec as P

BF = jnp.bfloat16
F32 = jnp.float32
MESH = pl.DeviceIdType.MESH


def repeat(count, step):
    if count <= 4:
        for i in range(count):
            step(i)
    else:
        lax.fori_loop(0, count, lambda i, c: (step(i), c)[1], 0)


def dot(a, b, ca, cb):
    return lax.dot_general(a, b, (((ca,), (cb,)), ((), ())), preferred_element_type=F32)


def eye(n):
    return lax.broadcasted_iota(jnp.int32, (n, n), 0) == lax.broadcasted_iota(jnp.int32, (n, n), 1)


def as_column(row):
    return jnp.sum(jnp.where(eye(row.shape[1]), row, 0.0), axis=1, keepdims=True)


def as_row(column):
    return jnp.sum(jnp.where(eye(column.shape[0]), column, 0.0), axis=0, keepdims=True)


def kernel(
    E, PN, cap, acts, cot, gates, owners, slots, win_h, wout_h, grads, gin_h, gout_h,
    win, wout, gin, gout, placing, zs_a, zs_g, gat_a, gat_g, xn, xg, inv_s, pre_s, slope_s, hid_s, bp_s,
    s_s, s_r, rs_s, rs_r, ret_s, ret_r, up_r, gate_s, inner_s, xn_t, hid_t, placing_t, win_t, wout_t,
    zsem_a, zrec_a, zsem_g, zrec_g, psem_a, prec_a, psem_g, prec_g,
    ssem, srec, rsem, rrec, tsem, trec, upsem, uprec, lsem, go_sem,
):
    seg = lax.axis_index("segment")
    me = lax.axis_index("expert")
    mp = lax.axis_index("pair")
    M, T, F = cot.shape
    D = F * PN
    H = win.shape[1]
    R = E * cap
    B = M * cap
    groups = min(E, 4)
    ge = E // groups
    mg = me // ge

    load_in = pltpu.make_async_copy(win_h.at[0, 0], win, lsem.at[0])
    load_out = pltpu.make_async_copy(wout_h.at[0, 0], wout, lsem.at[1])
    load_in.start()
    load_out.start()

    barrier = pltpu.get_barrier_semaphore()

    def greet_e(k):
        pl.semaphore_signal(barrier, inc=1, device_id={"expert": lax.rem(me + k + 1, E)}, device_id_type=MESH)

    repeat(E - 1, greet_e)
    for k in range(1, PN):
        pl.semaphore_signal(barrier, inc=1, device_id={"pair": lax.rem(mp + k, PN)}, device_id_type=MESH)
    pl.semaphore_signal(barrier, inc=1, device_id={"segment": 1 - seg}, device_id_type=MESH)

    for m in range(M):
        target = owners[seg, pl.ds(m, 1), :] * cap + slots[seg, pl.ds(m, 1), :]
        placing[m] = (lax.broadcasted_iota(jnp.int32, (R, T), 0) == target).astype(BF)

    def pack(values, zs):
        rows = [dot(placing[m], values[m], 1, 0) for m in range(M)]
        zs[...] = jnp.concatenate(rows, axis=1).astype(BF).reshape(E, cap, M * F)

    def z_copy(zs, gat, ssems, rsems, d, src):
        return pltpu.make_async_remote_copy(
            src_ref=zs.at[d], dst_ref=gat.at[mp, src], send_sem=ssems.at[d], recv_sem=rsems.at[src],
            device_id={"expert": d}, device_id_type=MESH)

    def send_z(zs, gat, ssems, rsems):
        repeat(E - 1, lambda k: z_copy(zs, gat, ssems, rsems, lax.rem(me + k + 1, E), me).start())
        gat[mp, me] = zs[me]

    def p_copy(gat, ssems, rsems, q, src, g):
        part = gat.at[src, pl.ds(g * ge, ge)]
        return pltpu.make_async_remote_copy(
            src_ref=part, dst_ref=part, send_sem=ssems.at[q, g], recv_sem=rsems.at[src, g],
            device_id={"pair": q}, device_id_type=MESH)

    def forward(zs, gat, zsems, zrecs, psems, precs, j):
        g = lax.rem(mg + groups - j, groups)

        def arrive(i):
            e = g * ge + i

            @pl.when(e != me)
            def _():
                z_copy(zs, gat, zsems, zrecs, e, e).wait_recv()

        repeat(ge, arrive)
        for k in range(PN - 1, 0, -1):
            p_copy(gat, psems, precs, lax.rem(mp + k, PN), mp, g).start()

    def turn_for(j):
        return lax.rem(mg + 2 * groups - 1 - j, groups)

    def gathered(gat, psems, precs, j):
        g = turn_for(j)
        for k in range(1, PN):
            q = lax.rem(mp + k, PN)
            p_copy(gat, psems, precs, q, q, g).wait_recv()
        return g

    def finish(zs, gat, zsems, zrecs, psems, precs):
        repeat(E - 1, lambda k: z_copy(zs, gat, zsems, zrecs, lax.rem(me + k + 1, E), me).wait_send())

        def one(g):
            for k in range(1, PN):
                p_copy(gat, psems, precs, lax.rem(mp + k, PN), mp, g).wait_send()

        repeat(groups, one)

    a_set = (zs_a, gat_a, zsem_a, zrec_a, psem_a, prec_a)
    g_set = (zs_g, gat_g, zsem_g, zrec_g, psem_g, prec_g)
    unit = ge * B

    def go(i):
        pl.semaphore_signal(go_sem.at[i], inc=1, device_id={"segment": 1 - seg}, device_id_type=MESH)

    def send_grad():
        scaled = [(gate_s[m] * up_r[m].astype(F32)).astype(BF) for m in range(M)]
        pack(scaled, zs_g)
        send_z(zs_g, gat_g, zsem_g, zrec_g)

    def take(gat, psems, precs, j, use):
        g = gathered(gat, psems, precs, j)

        def block(i):
            e = g * ge + i
            parts = [gat[q, e].astype(F32) for q in range(PN)]
            for m in range(M):
                full = jnp.concatenate([v[:, m * F:(m + 1) * F] for v in parts], axis=1)
                use(pl.ds(pl.multiple_of(e * B + m * cap, 16), cap), full)

        repeat(ge, block)
        return g, pl.ds(pl.multiple_of(g * unit, 16), unit)

    def norm_rows(rows, full):
        scale = lax.rsqrt(jnp.mean(full * full, axis=1, keepdims=True) + 1e-06)
        inv_s[rows, :] = scale
        xn[rows, :] = (full * scale).astype(BF)

    def grad_rows(rows, full):
        xg[rows, :] = full.astype(BF)

    def r_copy(q, src, g):
        rows = pl.ds(g * ge, ge)
        return pltpu.make_async_remote_copy(
            src_ref=rs_s.at[q, rows], dst_ref=rs_r.at[src, rows], send_sem=rsem.at[q, g], recv_sem=rrec.at[src, g],
            device_id={"pair": q}, device_id_type=MESH)

    def s_copy(q, src, g):
        rows = pl.ds(g * ge, ge)
        return pltpu.make_async_remote_copy(
            src_ref=s_s.at[rows], dst_ref=s_r.at[src, rows], send_sem=ssem.at[q, g], recv_sem=srec.at[src, g],
            device_id={"pair": q}, device_id_type=MESH)

    def forward_pass(j):
        _, rows = take(gat_a, psem_a, prec_a, j, norm_rows)
        for t in range(H // tile):
            col = pl.ds(t * tile, tile)
            u = dot(xn[rows, :], win[:, col], 1, 0)
            square = u * u
            tangent = jnp.tanh(0.7978845608 * (u + 0.044715 * square * u))
            pre_s[rows, col] = u.astype(BF)
            hid_s[rows, col] = (0.5 * u * (1.0 + tangent)).astype(BF)
            slope_s[rows, col] = 0.5 * (1.0 + tangent) + 0.5 * u * (1.0 - tangent * tangent) * 0.7978845608 * (
                1.0 + 0.134145 * square)

    def backward_pass(j):
        g, rows = take(gat_g, psem_g, prec_g, j, grad_rows)
        inner = jnp.zeros((unit, tile), F32)
        for t in range(H // tile):
            col = pl.ds(t * tile, tile)
            back = dot(xg[rows, :], wout_t[:, col], 1, 0)
            low = (back * slope_s[rows, col]).astype(BF)
            bp_s[rows, col] = low
            inner = inner + low.astype(F32) * pre_s[rows, col].astype(F32)
        inner_s[rows, :] = jnp.sum(inner, axis=1, keepdims=True)
        part = dot(bp_s[rows, :], win_t[...], 1, 0).reshape(ge, M, cap, D)
        for q in range(PN):
            joined = jnp.concatenate([part[:, m, :, q * F:(q + 1) * F] for m in range(M)], axis=-1)
            rs_s[q, pl.ds(g * ge, ge)] = joined.astype(BF)
        for k in range(PN - 1, 0, -1):
            r_copy(lax.rem(mp + k, PN), mp, g).start()

        def inner_row(i):
            e = g * ge + i
            row = as_row(inner_s[pl.ds(pl.multiple_of(e * B, 16), B), :])
            s_s[e] = row
            s_r[mp, e] = row

        repeat(ge, inner_row)
        for k in range(1, PN):
            s_copy(lax.rem(mp + k, PN), mp, g).start()
        rs_r[mp, pl.ds(g * ge, ge)] = rs_s[mp, pl.ds(g * ge, ge)]

    def turn():
        for t in range(D // 128):
            xn_t[pl.ds(t * 128, 128), :] = jnp.transpose(xn[:, pl.ds(t * 128, 128)])
        for t in range(H // 128):
            hid_t[pl.ds(t * 128, 128), :] = jnp.transpose(hid_s[:, pl.ds(t * 128, 128)])

    def first_grad():
        for t in range(H // tile):
            col = pl.ds(t * tile, tile)
            gin[:, col] = dot(xn_t[...], bp_s[:, col], 1, 0).astype(BF)
        put_in.start()

    def second_grad():
        for t in range(H // tile):
            col = pl.ds(t * tile, tile)
            gout[col, :] = dot(hid_t[col, :], xg[...], 1, 0).astype(BF)
        put_out.start()

    def t_copy(d, src):
        return pltpu.make_async_remote_copy(
            src_ref=ret_s.at[d], dst_ref=ret_r.at[src], send_sem=tsem.at[d], recv_sem=trec.at[src],
            device_id={"expert": d}, device_id_type=MESH)

    def give_back(j):
        g = turn_for(j)
        for k in range(1, PN):
            q = lax.rem(mp + k, PN)
            r_copy(q, q, g).wait_recv()
            s_copy(q, q, g).wait_recv()

        def block(i):
            e = g * ge + i
            total = rs_r[0, e].astype(F32)
            inner = s_r[0, e]
            for q in range(1, PN):
                total = total + rs_r[q, e].astype(F32)
                inner = inner + s_r[q, e]
            inner = as_column(inner)
            own = gat_a[mp, e].astype(F32)
            pieces = []
            for m in range(M):
                scale = inv_s[pl.ds(pl.multiple_of(e * B + m * cap, 16), cap), :]
                lanes = slice(m * F, (m + 1) * F)
                factor = scale * scale * inner[m * cap:(m + 1) * cap] / D
                pieces.append(scale * total[:, lanes] - factor * own[:, lanes])
            ret_s[e] = jnp.concatenate(pieces, axis=1).astype(BF)

            @pl.when(e != me)
            def _():
                t_copy(e, me).start()

        repeat(ge, block)

    def up_copy():
        return pltpu.make_async_remote_copy(
            src_ref=grads.at[0], dst_ref=up_r, send_sem=upsem, recv_sem=uprec,
            device_id={"segment": 1 - seg}, device_id_type=MESH)

    def cycle(step):
        lax.fori_loop(0, groups, lambda j, c: (step(j), c)[1], 0)

    put_in = pltpu.make_async_copy(gin, gin_h.at[0, 0], lsem.at[2])
    put_out = pltpu.make_async_copy(gout, gout_h.at[0, 0], lsem.at[3])
    tile = 256 if H % 256 == 0 else 128
    pack([acts[seg, m] for m in range(M)], zs_a)
    for m in range(M):
        gate_s[m] = as_column(gates[seg, pl.ds(m, 1), :])
        spot = owners[seg, pl.ds(m, 1), :] * cap + slots[seg, pl.ds(m, 1), :]
        spot = as_column(spot.astype(F32)).astype(jnp.int32)
        placing_t[m] = (lax.broadcasted_iota(jnp.int32, (T, R), 1) == spot).astype(BF)
    pl.semaphore_wait(barrier, E - 1 + PN - 1 + 1)

    @pl.when(seg == 0)
    def _():
        pl.semaphore_wait(go_sem.at[0], 1)

    send_z(zs_a, gat_a, zsem_a, zrec_a)

    @pl.when(seg == 1)
    def _():
        up_r[...] = cot[...]
        send_grad()

    load_in.wait()
    load_out.wait()

    def turn_weights(src, dst):
        for t in range(src.shape[1] // 128):
            col = pl.ds(t * 128, 128)
            dst[col, :] = jnp.transpose(src[:, col])

    @pl.when(seg == 0)
    def _():
        turn_weights(win, win_t)
        turn_weights(wout, wout_t)
        pl.semaphore_wait(go_sem.at[1], 1)

    def both(j):
        forward(*a_set, j)

        @pl.when(seg == 1)
        def _():
            forward(*g_set, j)
            if j == 0:
                turn_weights(win, win_t)
            if j == min(1, groups - 1):
                turn_weights(wout, wout_t)

    repeat(groups, both)

    @pl.when(seg == 1)
    def _():
        go(0)

    cycle(forward_pass)

    @pl.when(seg == 1)
    def _():
        go(1)

    @pl.when(seg == 0)
    def _():
        turn()
        up_copy().wait_recv()
        send_grad()
        repeat(groups, lambda j: forward(*g_set, j))

    def backward_and_back(j):
        backward_pass(j)

        @pl.when(j > 0)
        def _():
            give_back(j - 1)

    cycle(backward_and_back)

    @pl.when(seg == 0)
    def _():
        first_grad()

    give_back(groups - 1)
    ret_r[me] = ret_s[me]

    @pl.when(seg == 0)
    def _():
        second_grad()

    def back_arrive(k):
        src = lax.rem(me + k + 1, E)
        t_copy(src, src).wait_recv()

    repeat(E - 1, back_arrive)
    returned = ret_r[...].reshape(R, M * F)
    for m in range(M):
        restored = dot(placing_t[m], returned[:, m * F:(m + 1) * F], 1, 0)
        grads[0, m] = (up_r[m].astype(F32) + restored).astype(BF)

    @pl.when(seg == 1)
    def _():
        up_copy().start()
        turn()
        first_grad()
        second_grad()

    finish(*a_set)
    finish(*g_set)
    for k in range(1, PN):
        q = lax.rem(mp + k, PN)

        def sent(g):
            s_copy(q, mp, g).wait_send()
            r_copy(q, mp, g).wait_send()

        repeat(groups, sent)
    repeat(E - 1, lambda k: t_copy(lax.rem(me + k + 1, E), me).wait_send())
    put_in.wait()
    put_out.wait()

    @pl.when(seg == 1)
    def _():
        up_copy().wait_send()


def place_kernel(a, b, c, a_out, b_out, c_out, a_mid, b_mid, c_mid, in_sem, out_sem):
    moves = []
    for src, mid, dst, axis in ((a, a_mid, a_out, 1), (b, b_mid, b_out, 2), (c, c_mid, c_out, 2)):
        cuts = src.shape[1] if axis == 1 else 4
        step = src.shape[axis] // cuts
        for i in range(cuts):
            at = (slice(None),) * axis + (pl.ds(i * step, step),)
            n = len(moves)
            moves.append((
                pltpu.make_async_copy(src.at[at], mid.at[at], in_sem.at[n]),
                pltpu.make_async_copy(mid.at[at], dst.at[at], out_sem.at[n]),
            ))
    for first, _ in moves:
        first.start()
    for first, second in moves:
        first.wait()
        second.start()
    for _, second in moves:
        second.wait()


def body(acts, cotangent, gates, owners, slots, w_in, w_out):
    E = lax.axis_size("expert")
    PN = lax.axis_size("pair")
    M, T, F = cotangent.shape
    D, H = w_in.shape[2:]
    capacity = max(2, (5 * T + 4 * E - 1) // (4 * E))
    cap = (capacity + 15) // 16 * 16
    R = E * cap
    W = M * F
    groups = min(E, 4)
    vm = pltpu.VMEM
    dma = pltpu.SemaphoreType.DMA
    scratch = [
        vm((D, H), BF), vm((H, D), BF), vm((D, H), BF), vm((H, D), BF),
        vm((M, R, T), BF), vm((E, cap, W), BF), vm((E, cap, W), BF),
        vm((PN, E, cap, W), BF), vm((PN, E, cap, W), BF),
        vm((M * R, D), BF), vm((M * R, D), BF), vm((M * R, 1), F32),
        vm((M * R, H), BF), vm((M * R, H), F32), vm((M * R, H), BF), vm((M * R, H), BF),
        vm((E, 1, M * cap), F32), vm((PN, E, 1, M * cap), F32),
        vm((PN, E, cap, W), BF), vm((PN, E, cap, W), BF),
        vm((E, cap, W), BF), vm((E, cap, W), BF), vm((M, T, F), BF),
        vm((M, T, 1), F32), vm((M * R, 1), F32),
        vm((D, M * R), BF), vm((H, M * R), BF), vm((M, T, R), BF), vm((H, D), BF), vm((D, H), BF),
        dma((E,)), dma((E,)), dma((E,)), dma((E,)),
        dma((PN, groups)), dma((PN, groups)), dma((PN, groups)), dma((PN, groups)),
        dma((PN, groups)), dma((PN, groups)), dma((PN, groups)), dma((PN, groups)),
        dma((E,)), dma((E,)), dma(()), dma(()), dma((4,)), pltpu.SemaphoreType.REGULAR((2,)),
    ]
    whole = pl.BlockSpec(memory_space=pltpu.VMEM)
    away = pl.BlockSpec(memory_space=pl.ANY)
    shapes = (
            jax.ShapeDtypeStruct((1, M, T, F), BF),
            jax.ShapeDtypeStruct((1, 1, D, H), BF),
            jax.ShapeDtypeStruct((1, 1, H, D), BF),
    )
    held = pl.pallas_call(
        functools.partial(kernel, E, PN, cap),
        out_shape=shapes,
        in_specs=[whole] * 5 + [away] * 2,
        out_specs=(whole, away, away),
        scratch_shapes=scratch,
        compiler_params=pltpu.CompilerParams(
            collective_id=0, has_side_effects=True, vmem_limit_bytes=58 * 1024 * 1024),
        cost_estimate=pl.CostEstimate(
            flops=10 * M * R * D * H, bytes_accessed=8 * D * H, transcendentals=M * R * H),
    )(acts, cotangent, gates, owners, slots, w_in, w_out)
    return pl.pallas_call(
        place_kernel,
        out_shape=shapes,
        in_specs=[away] * 3,
        out_specs=(away,) * 3,
        scratch_shapes=[vm(x.shape, BF) for x in shapes] + [dma((M + 8,)), dma((M + 8,))],
        cost_estimate=pl.CostEstimate(flops=0, bytes_accessed=8 * D * H, transcendentals=0),
    )(*held)


def solution(mesh):
    placed = (
        P(None, None, "expert", "pair"),
        P(None, "expert", "pair"),
        P(None, None, "expert"),
        P(None, None, "expert"),
        P(None, None, "expert"),
        P("segment", "expert", None, "pair"),
        P("segment", "expert", "pair", None),
    )
    return jax.shard_map(
        body,
        mesh=mesh,
        in_specs=placed,
        out_specs=(
            P("segment", None, "expert", "pair"),
            P("segment", "expert", None, "pair"),
            P("segment", "expert", "pair", None),
        ),
        check_vma=False,
    )
```

```python
import functools

import jax
import jax.numpy as jnp
from jax import lax
from jax.experimental import pallas as pl
from jax.experimental.pallas import tpu as pltpu
from jax.sharding import PartitionSpec as P

BF = jnp.bfloat16
F32 = jnp.float32
MESH = pl.DeviceIdType.MESH


def repeat(count, step):
    if count <= 4:
        for i in range(count):
            step(i)
    else:
        lax.fori_loop(0, count, lambda i, c: (step(i), c)[1], 0)


def dot(a, b, ca, cb):
    return lax.dot_general(a, b, (((ca,), (cb,)), ((), ())), preferred_element_type=F32)


def eye(n):
    return lax.broadcasted_iota(jnp.int32, (n, n), 0) == lax.broadcasted_iota(jnp.int32, (n, n), 1)


def as_column(row):
    return jnp.sum(jnp.where(eye(row.shape[1]), row, 0.0), axis=1, keepdims=True)


def as_row(column):
    return jnp.sum(jnp.where(eye(column.shape[0]), column, 0.0), axis=0, keepdims=True)


def kernel(
    E, PN, cap, acts, cot, gates, owners, slots, win_h, wout_h, grads, gin_h, gout_h,
    win, wout, gin, gout, placing, zs_a, zs_g, gat_a, gat_g, xn, xg, inv_s, pre_s, slope_s, hid_s, bp_s,
    s_s, s_r, rs_s, rs_r, ret_s, ret_r, up_r, gate_s, inner_s, xn_t, hid_t, placing_t, win_t, wout_t,
    zsem_a, zrec_a, zsem_g, zrec_g, psem_a, prec_a, psem_g, prec_g,
    ssem, srec, rsem, rrec, tsem, trec, upsem, uprec, lsem, go_sem,
):
    seg = lax.axis_index("segment")
    me = lax.axis_index("expert")
    mp = lax.axis_index("pair")
    M, T, F = cot.shape
    D = F * PN
    H = win.shape[1]
    R = E * cap
    B = M * cap
    groups = min(E, 4)
    ge = E // groups
    mg = me // ge

    load_in = pltpu.make_async_copy(win_h.at[0, 0], win, lsem.at[0])
    load_out = pltpu.make_async_copy(wout_h.at[0, 0], wout, lsem.at[1])
    load_in.start()
    load_out.start()

    barrier = pltpu.get_barrier_semaphore()

    def greet_e(k):
        pl.semaphore_signal(barrier, inc=1, device_id={"expert": lax.rem(me + k + 1, E)}, device_id_type=MESH)

    repeat(E - 1, greet_e)
    for k in range(1, PN):
        pl.semaphore_signal(barrier, inc=1, device_id={"pair": lax.rem(mp + k, PN)}, device_id_type=MESH)
    pl.semaphore_signal(barrier, inc=1, device_id={"segment": 1 - seg}, device_id_type=MESH)

    for m in range(M):
        target = owners[seg, pl.ds(m, 1), :] * cap + slots[seg, pl.ds(m, 1), :]
        placing[m] = (lax.broadcasted_iota(jnp.int32, (R, T), 0) == target).astype(BF)

    def pack(values, zs):
        rows = [dot(placing[m], values[m], 1, 0) for m in range(M)]
        zs[...] = jnp.concatenate(rows, axis=1).astype(BF).reshape(E, cap, M * F)

    def z_copy(zs, gat, ssems, rsems, d, src):
        return pltpu.make_async_remote_copy(
            src_ref=zs.at[d], dst_ref=gat.at[mp, src], send_sem=ssems.at[d], recv_sem=rsems.at[src],
            device_id={"expert": d}, device_id_type=MESH)

    def send_z(zs, gat, ssems, rsems):
        repeat(E - 1, lambda k: z_copy(zs, gat, ssems, rsems, lax.rem(me + k + 1, E), me).start())
        gat[mp, me] = zs[me]

    def p_copy(gat, ssems, rsems, q, src, g):
        part = gat.at[src, pl.ds(g * ge, ge)]
        return pltpu.make_async_remote_copy(
            src_ref=part, dst_ref=part, send_sem=ssems.at[q, g], recv_sem=rsems.at[src, g],
            device_id={"pair": q}, device_id_type=MESH)

    def forward(zs, gat, zsems, zrecs, psems, precs, j):
        g = lax.rem(mg + groups - j, groups)

        def arrive(i):
            e = g * ge + i

            @pl.when(e != me)
            def _():
                z_copy(zs, gat, zsems, zrecs, e, e).wait_recv()

        repeat(ge, arrive)
        for k in range(PN - 1, 0, -1):
            p_copy(gat, psems, precs, lax.rem(mp + k, PN), mp, g).start()

    def turn_for(j):
        return lax.rem(mg + groups - j, groups)

    def gathered(gat, psems, precs, j):
        g = turn_for(j)
        for k in range(1, PN):
            q = lax.rem(mp + k, PN)
            p_copy(gat, psems, precs, q, q, g).wait_recv()
        return g

    def finish(zs, gat, zsems, zrecs, psems, precs):
        repeat(E - 1, lambda k: z_copy(zs, gat, zsems, zrecs, lax.rem(me + k + 1, E), me).wait_send())

        def one(g):
            for k in range(1, PN):
                p_copy(gat, psems, precs, lax.rem(mp + k, PN), mp, g).wait_send()

        repeat(groups, one)

    a_set = (zs_a, gat_a, zsem_a, zrec_a, psem_a, prec_a)
    g_set = (zs_g, gat_g, zsem_g, zrec_g, psem_g, prec_g)
    unit = ge * B

    def go(i):
        pl.semaphore_signal(go_sem.at[i], inc=1, device_id={"segment": 1 - seg}, device_id_type=MESH)

    def send_grad():
        scaled = [(gate_s[m] * up_r[m].astype(F32)).astype(BF) for m in range(M)]
        pack(scaled, zs_g)
        send_z(zs_g, gat_g, zsem_g, zrec_g)

    def take(gat, psems, precs, j, use):
        g = gathered(gat, psems, precs, j)

        def block(i):
            e = g * ge + i
            parts = [gat[q, e].astype(F32) for q in range(PN)]
            for m in range(M):
                full = jnp.concatenate([v[:, m * F:(m + 1) * F] for v in parts], axis=1)
                use(pl.ds(pl.multiple_of(e * B + m * cap, 16), cap), full)

        repeat(ge, block)
        return g, pl.ds(pl.multiple_of(g * unit, 16), unit)

    def norm_rows(rows, full):
        scale = lax.rsqrt(jnp.mean(full * full, axis=1, keepdims=True) + 1e-06)
        inv_s[rows, :] = scale
        xn[rows, :] = (full * scale).astype(BF)

    def grad_rows(rows, full):
        xg[rows, :] = full.astype(BF)

    def r_copy(q, src, g):
        rows = pl.ds(g * ge, ge)
        return pltpu.make_async_remote_copy(
            src_ref=rs_s.at[q, rows], dst_ref=rs_r.at[src, rows], send_sem=rsem.at[q, g], recv_sem=rrec.at[src, g],
            device_id={"pair": q}, device_id_type=MESH)

    def s_copy(q, src, g):
        rows = pl.ds(g * ge, ge)
        return pltpu.make_async_remote_copy(
            src_ref=s_s.at[rows], dst_ref=s_r.at[src, rows], send_sem=ssem.at[q, g], recv_sem=srec.at[src, g],
            device_id={"pair": q}, device_id_type=MESH)

    def forward_pass(j):
        _, rows = take(gat_a, psem_a, prec_a, j, norm_rows)
        for t in range(H // tile):
            col = pl.ds(t * tile, tile)
            u = dot(xn[rows, :], win[:, col], 1, 0)
            square = u * u
            tangent = jnp.tanh(0.7978845608 * (u + 0.044715 * square * u))
            pre_s[rows, col] = u.astype(BF)
            hid_s[rows, col] = (0.5 * u * (1.0 + tangent)).astype(BF)
            slope_s[rows, col] = 0.5 * (1.0 + tangent) + 0.5 * u * (1.0 - tangent * tangent) * 0.7978845608 * (
                1.0 + 0.134145 * square)

    def backward_pass(j):
        g, rows = take(gat_g, psem_g, prec_g, j, grad_rows)
        inner = jnp.zeros((unit, tile), F32)
        for t in range(H // tile):
            col = pl.ds(t * tile, tile)
            back = dot(xg[rows, :], wout_t[:, col], 1, 0)
            low = (back * slope_s[rows, col]).astype(BF)
            bp_s[rows, col] = low
            inner = inner + low.astype(F32) * pre_s[rows, col].astype(F32)
        inner_s[rows, :] = jnp.sum(inner, axis=1, keepdims=True)
        part = dot(bp_s[rows, :], win_t[...], 1, 0).reshape(ge, M, cap, D)
        for q in range(PN):
            joined = jnp.concatenate([part[:, m, :, q * F:(q + 1) * F] for m in range(M)], axis=-1)
            rs_s[q, pl.ds(g * ge, ge)] = joined.astype(BF)
        for k in range(PN - 1, 0, -1):
            r_copy(lax.rem(mp + k, PN), mp, g).start()

        def inner_row(i):
            e = g * ge + i
            row = as_row(inner_s[pl.ds(pl.multiple_of(e * B, 16), B), :])
            s_s[e] = row
            s_r[mp, e] = row

        repeat(ge, inner_row)
        for k in range(1, PN):
            s_copy(lax.rem(mp + k, PN), mp, g).start()
        rs_r[mp, pl.ds(g * ge, ge)] = rs_s[mp, pl.ds(g * ge, ge)]

    def turn():
        for t in range(D // 128):
            xn_t[pl.ds(t * 128, 128), :] = jnp.transpose(xn[:, pl.ds(t * 128, 128)])
        for t in range(H // 128):
            hid_t[pl.ds(t * 128, 128), :] = jnp.transpose(hid_s[:, pl.ds(t * 128, 128)])

    def first_grad():
        for t in range(H // tile):
            col = pl.ds(t * tile, tile)
            gin[:, col] = dot(xn_t[...], bp_s[:, col], 1, 0).astype(BF)
        put_in.start()

    def second_grad():
        for t in range(H // tile):
            col = pl.ds(t * tile, tile)
            gout[col, :] = dot(hid_t[col, :], xg[...], 1, 0).astype(BF)
        put_out.start()

    def t_copy(d, src):
        return pltpu.make_async_remote_copy(
            src_ref=ret_s.at[d], dst_ref=ret_r.at[src], send_sem=tsem.at[d], recv_sem=trec.at[src],
            device_id={"expert": d}, device_id_type=MESH)

    def give_back(j):
        g = turn_for(j)
        for k in range(1, PN):
            q = lax.rem(mp + k, PN)
            r_copy(q, q, g).wait_recv()
            s_copy(q, q, g).wait_recv()

        def block(i):
            e = g * ge + i
            total = rs_r[0, e].astype(F32)
            inner = s_r[0, e]
            for q in range(1, PN):
                total = total + rs_r[q, e].astype(F32)
                inner = inner + s_r[q, e]
            inner = as_column(inner)
            own = gat_a[mp, e].astype(F32)
            pieces = []
            for m in range(M):
                scale = inv_s[pl.ds(pl.multiple_of(e * B + m * cap, 16), cap), :]
                lanes = slice(m * F, (m + 1) * F)
                factor = scale * scale * inner[m * cap:(m + 1) * cap] / D
                pieces.append(scale * total[:, lanes] - factor * own[:, lanes])
            ret_s[e] = jnp.concatenate(pieces, axis=1).astype(BF)

            @pl.when(e != me)
            def _():
                t_copy(e, me).start()

        repeat(ge, block)

    def up_copy():
        return pltpu.make_async_remote_copy(
            src_ref=grads.at[0], dst_ref=up_r, send_sem=upsem, recv_sem=uprec,
            device_id={"segment": 1 - seg}, device_id_type=MESH)

    def cycle(step):
        lax.fori_loop(0, groups, lambda j, c: (step(j), c)[1], 0)

    put_in = pltpu.make_async_copy(gin, gin_h.at[0, 0], lsem.at[2])
    put_out = pltpu.make_async_copy(gout, gout_h.at[0, 0], lsem.at[3])
    tile = 256 if H % 256 == 0 else 128
    pack([acts[seg, m] for m in range(M)], zs_a)
    for m in range(M):
        gate_s[m] = as_column(gates[seg, pl.ds(m, 1), :])
        spot = owners[seg, pl.ds(m, 1), :] * cap + slots[seg, pl.ds(m, 1), :]
        spot = as_column(spot.astype(F32)).astype(jnp.int32)
        placing_t[m] = (lax.broadcasted_iota(jnp.int32, (T, R), 1) == spot).astype(BF)
    pl.semaphore_wait(barrier, E - 1 + PN - 1 + 1)

    @pl.when(seg == 0)
    def _():
        pl.semaphore_wait(go_sem.at[0], 1)

    send_z(zs_a, gat_a, zsem_a, zrec_a)

    @pl.when(seg == 1)
    def _():
        up_r[...] = cot[...]
        send_grad()

    load_in.wait()
    load_out.wait()

    def turn_weights(src, dst):
        for t in range(src.shape[1] // 128):
            col = pl.ds(t * 128, 128)
            dst[col, :] = jnp.transpose(src[:, col])

    @pl.when(seg == 0)
    def _():
        turn_weights(win, win_t)
        turn_weights(wout, wout_t)
        pl.semaphore_wait(go_sem.at[1], 1)

    def both(j):
        forward(*a_set, j)

        @pl.when(seg == 1)
        def _():
            forward(*g_set, j)
            if j == 0:
                turn_weights(win, win_t)
            if j == min(1, groups - 1):
                turn_weights(wout, wout_t)

    repeat(groups, both)

    @pl.when(seg == 1)
    def _():
        go(0)

    cycle(forward_pass)

    @pl.when(seg == 0)
    def _():
        turn()
        up_copy().wait_recv()
        send_grad()
        repeat(groups, lambda j: forward(*g_set, j))

    def backward_and_back(j):
        backward_pass(j)

        @pl.when((seg == 1) & (j == groups // 2))
        def _():
            go(1)

        @pl.when(j >= lag)
        def _():
            give_back(j - lag)

    lag = min(2, groups)
    cycle(backward_and_back)
    if lag == 2:
        give_back(groups - 2)

    @pl.when(seg == 0)
    def _():
        first_grad()

    give_back(groups - 1)
    ret_r[me] = ret_s[me]

    @pl.when(seg == 0)
    def _():
        second_grad()

    def back_arrive(k):
        src = lax.rem(me + k + 1, E)
        t_copy(src, src).wait_recv()

    repeat(E - 1, back_arrive)
    returned = ret_r[...].reshape(R, M * F)
    for m in range(M):
        restored = dot(placing_t[m], returned[:, m * F:(m + 1) * F], 1, 0)
        grads[0, m] = (up_r[m].astype(F32) + restored).astype(BF)

    @pl.when(seg == 1)
    def _():
        up_copy().start()
        turn()
        first_grad()
        second_grad()

    finish(*a_set)
    finish(*g_set)
    for k in range(1, PN):
        q = lax.rem(mp + k, PN)

        def sent(g):
            s_copy(q, mp, g).wait_send()
            r_copy(q, mp, g).wait_send()

        repeat(groups, sent)
    repeat(E - 1, lambda k: t_copy(lax.rem(me + k + 1, E), me).wait_send())
    put_in.wait()
    put_out.wait()

    @pl.when(seg == 1)
    def _():
        up_copy().wait_send()


def place_kernel(a, b, c, a_out, b_out, c_out, a_mid, b_mid, c_mid, in_sem, out_sem):
    moves = []
    for src, mid, dst, axis in ((a, a_mid, a_out, 1), (b, b_mid, b_out, 2), (c, c_mid, c_out, 2)):
        cuts = src.shape[1] if axis == 1 else 4
        step = src.shape[axis] // cuts
        for i in range(cuts):
            at = (slice(None),) * axis + (pl.ds(i * step, step),)
            n = len(moves)
            moves.append((
                pltpu.make_async_copy(src.at[at], mid.at[at], in_sem.at[n]),
                pltpu.make_async_copy(mid.at[at], dst.at[at], out_sem.at[n]),
            ))
    for first, _ in moves:
        first.start()
    for first, second in moves:
        first.wait()
        second.start()
    for _, second in moves:
        second.wait()


def body(acts, cotangent, gates, owners, slots, w_in, w_out):
    E = lax.axis_size("expert")
    PN = lax.axis_size("pair")
    M, T, F = cotangent.shape
    D, H = w_in.shape[2:]
    capacity = max(2, (5 * T + 4 * E - 1) // (4 * E))
    cap = (capacity + 15) // 16 * 16
    R = E * cap
    W = M * F
    groups = min(E, 4)
    vm = pltpu.VMEM
    dma = pltpu.SemaphoreType.DMA
    scratch = [
        vm((D, H), BF), vm((H, D), BF), vm((D, H), BF), vm((H, D), BF),
        vm((M, R, T), BF), vm((E, cap, W), BF), vm((E, cap, W), BF),
        vm((PN, E, cap, W), BF), vm((PN, E, cap, W), BF),
        vm((M * R, D), BF), vm((M * R, D), BF), vm((M * R, 1), F32),
        vm((M * R, H), BF), vm((M * R, H), F32), vm((M * R, H), BF), vm((M * R, H), BF),
        vm((E, 1, M * cap), F32), vm((PN, E, 1, M * cap), F32),
        vm((PN, E, cap, W), BF), vm((PN, E, cap, W), BF),
        vm((E, cap, W), BF), vm((E, cap, W), BF), vm((M, T, F), BF),
        vm((M, T, 1), F32), vm((M * R, 1), F32),
        vm((D, M * R), BF), vm((H, M * R), BF), vm((M, T, R), BF), vm((H, D), BF), vm((D, H), BF),
        dma((E,)), dma((E,)), dma((E,)), dma((E,)),
        dma((PN, groups)), dma((PN, groups)), dma((PN, groups)), dma((PN, groups)),
        dma((PN, groups)), dma((PN, groups)), dma((PN, groups)), dma((PN, groups)),
        dma((E,)), dma((E,)), dma(()), dma(()), dma((4,)), pltpu.SemaphoreType.REGULAR((2,)),
    ]
    whole = pl.BlockSpec(memory_space=pltpu.VMEM)
    away = pl.BlockSpec(memory_space=pl.ANY)
    shapes = (
            jax.ShapeDtypeStruct((1, M, T, F), BF),
            jax.ShapeDtypeStruct((1, 1, D, H), BF),
            jax.ShapeDtypeStruct((1, 1, H, D), BF),
    )
    held = pl.pallas_call(
        functools.partial(kernel, E, PN, cap),
        out_shape=shapes,
        in_specs=[whole] * 5 + [away] * 2,
        out_specs=(whole, away, away),
        scratch_shapes=scratch,
        compiler_params=pltpu.CompilerParams(
            collective_id=0, has_side_effects=True, vmem_limit_bytes=58 * 1024 * 1024),
        cost_estimate=pl.CostEstimate(
            flops=10 * M * R * D * H, bytes_accessed=8 * D * H, transcendentals=M * R * H),
    )(acts, cotangent, gates, owners, slots, w_in, w_out)
    return pl.pallas_call(
        place_kernel,
        out_shape=shapes,
        in_specs=[away] * 3,
        out_specs=(away,) * 3,
        scratch_shapes=[vm(x.shape, BF) for x in shapes] + [dma((M + 8,)), dma((M + 8,))],
        cost_estimate=pl.CostEstimate(flops=0, bytes_accessed=8 * D * H, transcendentals=0),
    )(*held)


def solution(mesh):
    placed = (
        P(None, None, "expert", "pair"),
        P(None, "expert", "pair"),
        P(None, None, "expert"),
        P(None, None, "expert"),
        P(None, None, "expert"),
        P("segment", "expert", None, "pair"),
        P("segment", "expert", "pair", None),
    )
    return jax.shard_map(
        body,
        mesh=mesh,
        in_specs=placed,
        out_specs=(
            P("segment", None, "expert", "pair"),
            P("segment", "expert", None, "pair"),
            P("segment", "expert", "pair", None),
        ),
        check_vma=False,
    )
```

```python
import functools

import jax
import jax.numpy as jnp
from jax import lax
from jax.experimental import pallas as pl
from jax.experimental.pallas import tpu as pltpu
from jax.sharding import PartitionSpec as P

BF = jnp.bfloat16
F32 = jnp.float32
MESH = pl.DeviceIdType.MESH


def repeat(count, step):
    if count <= 4:
        for i in range(count):
            step(i)
    else:
        lax.fori_loop(0, count, lambda i, c: (step(i), c)[1], 0)


def dot(a, b, ca, cb):
    return lax.dot_general(a, b, (((ca,), (cb,)), ((), ())), preferred_element_type=F32)


def eye(n):
    return lax.broadcasted_iota(jnp.int32, (n, n), 0) == lax.broadcasted_iota(jnp.int32, (n, n), 1)


def as_column(row):
    return jnp.sum(jnp.where(eye(row.shape[1]), row, 0.0), axis=1, keepdims=True)


def as_row(column):
    return jnp.sum(jnp.where(eye(column.shape[0]), column, 0.0), axis=0, keepdims=True)


def kernel(
    E, PN, cap, acts, cot, gates, owners, slots, win_h, wout_h, grads, gin_h, gout_h,
    win, wout, gin, gout, placing, zs_a, zs_g, gat_a, gat_g, xn, xg, inv_s, pre_s, slope_s, hid_s, bp_s,
    s_s, s_r, rs_s, rs_r, ret_s, ret_r, up_r, gate_s, inner_s, xn_t, hid_t, placing_t, win_t, wout_t,
    zsem_a, zrec_a, zsem_g, zrec_g, psem_a, prec_a, psem_g, prec_g,
    ssem, srec, rsem, rrec, tsem, trec, upsem, uprec, lsem, go_sem,
):
    seg = lax.axis_index("segment")
    me = lax.axis_index("expert")
    mp = lax.axis_index("pair")
    M, T, F = cot.shape
    D = F * PN
    H = win.shape[1]
    R = E * cap
    B = M * cap
    groups = min(E, 4)
    ge = E // groups
    mg = me // ge

    load_in = pltpu.make_async_copy(win_h.at[0, 0], win, lsem.at[0])
    load_out = pltpu.make_async_copy(wout_h.at[0, 0], wout, lsem.at[1])
    load_in.start()
    load_out.start()

    barrier = pltpu.get_barrier_semaphore()

    def greet_e(k):
        pl.semaphore_signal(barrier, inc=1, device_id={"expert": lax.rem(me + k + 1, E)}, device_id_type=MESH)

    repeat(E - 1, greet_e)
    for k in range(1, PN):
        pl.semaphore_signal(barrier, inc=1, device_id={"pair": lax.rem(mp + k, PN)}, device_id_type=MESH)
    pl.semaphore_signal(barrier, inc=1, device_id={"segment": 1 - seg}, device_id_type=MESH)

    for m in range(M):
        target = owners[seg, pl.ds(m, 1), :] * cap + slots[seg, pl.ds(m, 1), :]
        placing[m] = (lax.broadcasted_iota(jnp.int32, (R, T), 0) == target).astype(BF)

    def pack(values, zs):
        rows = [dot(placing[m], values[m], 1, 0) for m in range(M)]
        zs[...] = jnp.concatenate(rows, axis=1).astype(BF).reshape(E, cap, M * F)

    def z_copy(zs, gat, ssems, rsems, d, src):
        return pltpu.make_async_remote_copy(
            src_ref=zs.at[d], dst_ref=gat.at[mp, src], send_sem=ssems.at[d], recv_sem=rsems.at[src],
            device_id={"expert": d}, device_id_type=MESH)

    def send_z(zs, gat, ssems, rsems):
        repeat(E - 1, lambda k: z_copy(zs, gat, ssems, rsems, lax.rem(me + k + 1, E), me).start())
        gat[mp, me] = zs[me]

    def p_copy(gat, ssems, rsems, q, src, g):
        part = gat.at[src, pl.ds(g * ge, ge)]
        return pltpu.make_async_remote_copy(
            src_ref=part, dst_ref=part, send_sem=ssems.at[q, g], recv_sem=rsems.at[src, g],
            device_id={"pair": q}, device_id_type=MESH)

    def forward(zs, gat, zsems, zrecs, psems, precs, j):
        g = lax.rem(mg + groups - j, groups)

        def arrive(i):
            e = g * ge + i

            @pl.when(e != me)
            def _():
                z_copy(zs, gat, zsems, zrecs, e, e).wait_recv()

        repeat(ge, arrive)
        for k in range(PN - 1, 0, -1):
            p_copy(gat, psems, precs, lax.rem(mp + k, PN), mp, g).start()

    def gathered(gat, psems, precs, j):
        g = lax.rem(mg + groups - j, groups)
        for k in range(1, PN):
            q = lax.rem(mp + k, PN)
            p_copy(gat, psems, precs, q, q, g).wait_recv()
        return g

    def finish(zs, gat, zsems, zrecs, psems, precs):
        repeat(E - 1, lambda k: z_copy(zs, gat, zsems, zrecs, lax.rem(me + k + 1, E), me).wait_send())

        def one(g):
            for k in range(1, PN):
                p_copy(gat, psems, precs, lax.rem(mp + k, PN), mp, g).wait_send()

        repeat(groups, one)

    a_set = (zs_a, gat_a, zsem_a, zrec_a, psem_a, prec_a)
    g_set = (zs_g, gat_g, zsem_g, zrec_g, psem_g, prec_g)
    unit = ge * B

    def go(i):
        pl.semaphore_signal(go_sem.at[i], inc=1, device_id={"segment": 1 - seg}, device_id_type=MESH)

    def send_grad():
        scaled = [(gate_s[m] * up_r[m].astype(F32)).astype(BF) for m in range(M)]
        pack(scaled, zs_g)
        send_z(zs_g, gat_g, zsem_g, zrec_g)

    def take(gat, psems, precs, j, use):
        g = gathered(gat, psems, precs, j)

        def block(i):
            e = g * ge + i
            parts = [gat[q, e].astype(F32) for q in range(PN)]
            for m in range(M):
                full = jnp.concatenate([v[:, m * F:(m + 1) * F] for v in parts], axis=1)
                use(pl.ds(pl.multiple_of(e * B + m * cap, 16), cap), full)

        repeat(ge, block)
        return g, pl.ds(pl.multiple_of(g * unit, 16), unit)

    def norm_rows(rows, full):
        scale = lax.rsqrt(jnp.mean(full * full, axis=1, keepdims=True) + 1e-06)
        inv_s[rows, :] = scale
        xn[rows, :] = (full * scale).astype(BF)

    def grad_rows(rows, full):
        xg[rows, :] = full.astype(BF)

    def r_copy(q, src, g):
        rows = pl.ds(g * ge, ge)
        return pltpu.make_async_remote_copy(
            src_ref=rs_s.at[q, rows], dst_ref=rs_r.at[src, rows], send_sem=rsem.at[q, g], recv_sem=rrec.at[src, g],
            device_id={"pair": q}, device_id_type=MESH)

    def s_copy(q, src, g):
        rows = pl.ds(g * ge, ge)
        return pltpu.make_async_remote_copy(
            src_ref=s_s.at[rows], dst_ref=s_r.at[src, rows], send_sem=ssem.at[q, g], recv_sem=srec.at[src, g],
            device_id={"pair": q}, device_id_type=MESH)

    def forward_pass(j):
        _, rows = take(gat_a, psem_a, prec_a, j, norm_rows)
        for t in range(H // tile):
            col = pl.ds(t * tile, tile)
            u = dot(xn[rows, :], win[:, col], 1, 0)
            square = u * u
            tangent = jnp.tanh(0.7978845608 * (u + 0.044715 * square * u))
            pre_s[rows, col] = u.astype(BF)
            hid_s[rows, col] = (0.5 * u * (1.0 + tangent)).astype(BF)
            slope_s[rows, col] = 0.5 * (1.0 + tangent) + 0.5 * u * (1.0 - tangent * tangent) * 0.7978845608 * (
                1.0 + 0.134145 * square)

    def backward_pass(j):
        g, rows = take(gat_g, psem_g, prec_g, j, grad_rows)
        inner = jnp.zeros((unit, tile), F32)
        for t in range(H // tile):
            col = pl.ds(t * tile, tile)
            back = dot(xg[rows, :], wout_t[:, col], 1, 0)
            low = (back * slope_s[rows, col]).astype(BF)
            bp_s[rows, col] = low
            inner = inner + low.astype(F32) * pre_s[rows, col].astype(F32)
        inner_s[rows, :] = jnp.sum(inner, axis=1, keepdims=True)
        part = dot(bp_s[rows, :], win_t[...], 1, 0).reshape(ge, M, cap, D)
        for q in range(PN):
            joined = jnp.concatenate([part[:, m, :, q * F:(q + 1) * F] for m in range(M)], axis=-1)
            rs_s[q, pl.ds(g * ge, ge)] = joined.astype(BF)
        for k in range(PN - 1, 0, -1):
            r_copy(lax.rem(mp + k, PN), mp, g).start()

        def inner_row(i):
            e = g * ge + i
            row = as_row(inner_s[pl.ds(pl.multiple_of(e * B, 16), B), :])
            s_s[e] = row
            s_r[mp, e] = row

        repeat(ge, inner_row)
        for k in range(1, PN):
            s_copy(lax.rem(mp + k, PN), mp, g).start()
        rs_r[mp, pl.ds(g * ge, ge)] = rs_s[mp, pl.ds(g * ge, ge)]

    def turn():
        for t in range(D // 128):
            xn_t[pl.ds(t * 128, 128), :] = jnp.transpose(xn[:, pl.ds(t * 128, 128)])
        for t in range(H // 128):
            hid_t[pl.ds(t * 128, 128), :] = jnp.transpose(hid_s[:, pl.ds(t * 128, 128)])

    def first_grad():
        for t in range(H // tile):
            col = pl.ds(t * tile, tile)
            gin[:, col] = dot(xn_t[...], bp_s[:, col], 1, 0).astype(BF)
        put_in.start()

    def second_grad():
        for t in range(H // tile):
            col = pl.ds(t * tile, tile)
            gout[col, :] = dot(hid_t[col, :], xg[...], 1, 0).astype(BF)
        put_out.start()

    def t_copy(d, src):
        return pltpu.make_async_remote_copy(
            src_ref=ret_s.at[d], dst_ref=ret_r.at[src], send_sem=tsem.at[d], recv_sem=trec.at[src],
            device_id={"expert": d}, device_id_type=MESH)

    def give_back(j):
        g = lax.rem(mg + groups - j, groups)
        for k in range(1, PN):
            q = lax.rem(mp + k, PN)
            r_copy(q, q, g).wait_recv()
            s_copy(q, q, g).wait_recv()

        def block(i):
            e = g * ge + i
            total = rs_r[0, e].astype(F32)
            inner = s_r[0, e]
            for q in range(1, PN):
                total = total + rs_r[q, e].astype(F32)
                inner = inner + s_r[q, e]
            inner = as_column(inner)
            own = gat_a[mp, e].astype(F32)
            pieces = []
            for m in range(M):
                scale = inv_s[pl.ds(pl.multiple_of(e * B + m * cap, 16), cap), :]
                lanes = slice(m * F, (m + 1) * F)
                factor = scale * scale * inner[m * cap:(m + 1) * cap] / D
                pieces.append(scale * total[:, lanes] - factor * own[:, lanes])
            ret_s[e] = jnp.concatenate(pieces, axis=1).astype(BF)

            @pl.when(e != me)
            def _():
                t_copy(e, me).start()

        repeat(ge, block)

    def up_copy():
        return pltpu.make_async_remote_copy(
            src_ref=grads.at[0], dst_ref=up_r, send_sem=upsem, recv_sem=uprec,
            device_id={"segment": 1 - seg}, device_id_type=MESH)

    def cycle(step):
        lax.fori_loop(0, groups, lambda j, c: (step(j), c)[1], 0)

    put_in = pltpu.make_async_copy(gin, gin_h.at[0, 0], lsem.at[2])
    put_out = pltpu.make_async_copy(gout, gout_h.at[0, 0], lsem.at[3])
    tile = 256 if H % 256 == 0 else 128
    pack([acts[seg, m] for m in range(M)], zs_a)
    for m in range(M):
        gate_s[m] = as_column(gates[seg, pl.ds(m, 1), :])
        spot = owners[seg, pl.ds(m, 1), :] * cap + slots[seg, pl.ds(m, 1), :]
        spot = as_column(spot.astype(F32)).astype(jnp.int32)
        placing_t[m] = (lax.broadcasted_iota(jnp.int32, (T, R), 1) == spot).astype(BF)
    pl.semaphore_wait(barrier, E - 1 + PN - 1 + 1)

    @pl.when(seg == 0)
    def _():
        pl.semaphore_wait(go_sem.at[0], 1)

    send_z(zs_a, gat_a, zsem_a, zrec_a)

    @pl.when(seg == 1)
    def _():
        up_r[...] = cot[...]
        send_grad()

    load_in.wait()
    load_out.wait()
    for t in range(H // 128):
        col = pl.ds(t * 128, 128)
        win_t[col, :] = jnp.transpose(win[:, col])
    for t in range(D // 128):
        col = pl.ds(t * 128, 128)
        wout_t[col, :] = jnp.transpose(wout[:, col])

    @pl.when(seg == 0)
    def _():
        pl.semaphore_wait(go_sem.at[1], 1)

    def both(j):
        forward(*a_set, j)

        @pl.when(seg == 1)
        def _():
            forward(*g_set, j)

    repeat(groups, both)

    @pl.when(seg == 1)
    def _():
        go(0)

    cycle(forward_pass)

    @pl.when(seg == 0)
    def _():
        turn()
        up_copy().wait_recv()
        send_grad()
        repeat(groups, lambda j: forward(*g_set, j))

    cycle(backward_pass)

    @pl.when(seg == 1)
    def _():
        go(1)

    cycle(give_back)
    ret_r[me] = ret_s[me]

    @pl.when(seg == 0)
    def _():
        first_grad()
        second_grad()

    def back_arrive(k):
        src = lax.rem(me + k + 1, E)
        t_copy(src, src).wait_recv()

    repeat(E - 1, back_arrive)
    returned = ret_r[...].reshape(R, M * F)
    for m in range(M):
        restored = dot(placing_t[m], returned[:, m * F:(m + 1) * F], 1, 0)
        grads[0, m] = (up_r[m].astype(F32) + restored).astype(BF)

    @pl.when(seg == 1)
    def _():
        up_copy().start()
        turn()
        first_grad()
        second_grad()

    finish(*a_set)
    finish(*g_set)
    for k in range(1, PN):
        q = lax.rem(mp + k, PN)

        def sent(g):
            s_copy(q, mp, g).wait_send()
            r_copy(q, mp, g).wait_send()

        repeat(groups, sent)
    repeat(E - 1, lambda k: t_copy(lax.rem(me + k + 1, E), me).wait_send())
    put_in.wait()
    put_out.wait()

    @pl.when(seg == 1)
    def _():
        up_copy().wait_send()


def place_kernel(a, b, c, a_out, b_out, c_out, a_mid, b_mid, c_mid, in_sem, out_sem):
    moves = []
    for src, mid, dst, axis in ((a, a_mid, a_out, 1), (b, b_mid, b_out, 2), (c, c_mid, c_out, 2)):
        cuts = src.shape[1] if axis == 1 else 4
        step = src.shape[axis] // cuts
        for i in range(cuts):
            at = (slice(None),) * axis + (pl.ds(i * step, step),)
            n = len(moves)
            moves.append((
                pltpu.make_async_copy(src.at[at], mid.at[at], in_sem.at[n]),
                pltpu.make_async_copy(mid.at[at], dst.at[at], out_sem.at[n]),
            ))
    for first, _ in moves:
        first.start()
    for first, second in moves:
        first.wait()
        second.start()
    for _, second in moves:
        second.wait()


def body(acts, cotangent, gates, owners, slots, w_in, w_out):
    E = lax.axis_size("expert")
    PN = lax.axis_size("pair")
    M, T, F = cotangent.shape
    D, H = w_in.shape[2:]
    capacity = max(2, (5 * T + 4 * E - 1) // (4 * E))
    cap = (capacity + 15) // 16 * 16
    R = E * cap
    W = M * F
    groups = min(E, 4)
    vm = pltpu.VMEM
    dma = pltpu.SemaphoreType.DMA
    scratch = [
        vm((D, H), BF), vm((H, D), BF), vm((D, H), BF), vm((H, D), BF),
        vm((M, R, T), BF), vm((E, cap, W), BF), vm((E, cap, W), BF),
        vm((PN, E, cap, W), BF), vm((PN, E, cap, W), BF),
        vm((M * R, D), BF), vm((M * R, D), BF), vm((M * R, 1), F32),
        vm((M * R, H), BF), vm((M * R, H), F32), vm((M * R, H), BF), vm((M * R, H), BF),
        vm((E, 1, M * cap), F32), vm((PN, E, 1, M * cap), F32),
        vm((PN, E, cap, W), BF), vm((PN, E, cap, W), BF),
        vm((E, cap, W), BF), vm((E, cap, W), BF), vm((M, T, F), BF),
        vm((M, T, 1), F32), vm((M * R, 1), F32),
        vm((D, M * R), BF), vm((H, M * R), BF), vm((M, T, R), BF), vm((H, D), BF), vm((D, H), BF),
        dma((E,)), dma((E,)), dma((E,)), dma((E,)),
        dma((PN, groups)), dma((PN, groups)), dma((PN, groups)), dma((PN, groups)),
        dma((PN, groups)), dma((PN, groups)), dma((PN, groups)), dma((PN, groups)),
        dma((E,)), dma((E,)), dma(()), dma(()), dma((4,)), pltpu.SemaphoreType.REGULAR((2,)),
    ]
    whole = pl.BlockSpec(memory_space=pltpu.VMEM)
    away = pl.BlockSpec(memory_space=pl.ANY)
    shapes = (
            jax.ShapeDtypeStruct((1, M, T, F), BF),
            jax.ShapeDtypeStruct((1, 1, D, H), BF),
            jax.ShapeDtypeStruct((1, 1, H, D), BF),
    )
    held = pl.pallas_call(
        functools.partial(kernel, E, PN, cap),
        out_shape=shapes,
        in_specs=[whole] * 5 + [away] * 2,
        out_specs=(whole, away, away),
        scratch_shapes=scratch,
        compiler_params=pltpu.CompilerParams(
            collective_id=0, has_side_effects=True, vmem_limit_bytes=58 * 1024 * 1024),
        cost_estimate=pl.CostEstimate(
            flops=10 * M * R * D * H, bytes_accessed=8 * D * H, transcendentals=M * R * H),
    )(acts, cotangent, gates, owners, slots, w_in, w_out)
    return pl.pallas_call(
        place_kernel,
        out_shape=shapes,
        in_specs=[away] * 3,
        out_specs=(away,) * 3,
        scratch_shapes=[vm(x.shape, BF) for x in shapes] + [dma((M + 8,)), dma((M + 8,))],
        cost_estimate=pl.CostEstimate(flops=0, bytes_accessed=8 * D * H, transcendentals=0),
    )(*held)


def solution(mesh):
    placed = (
        P(None, None, "expert", "pair"),
        P(None, "expert", "pair"),
        P(None, None, "expert"),
        P(None, None, "expert"),
        P(None, None, "expert"),
        P("segment", "expert", None, "pair"),
        P("segment", "expert", "pair", None),
    )
    return jax.shard_map(
        body,
        mesh=mesh,
        in_specs=placed,
        out_specs=(
            P("segment", None, "expert", "pair"),
            P("segment", "expert", None, "pair"),
            P("segment", "expert", "pair", None),
        ),
        check_vma=False,
    )
```
